128 devices in a mesh: fsdp: 128 (over y, z, x, core).
Axes of the slice: x: 4, y: 4, z: 4, core: 2. Of those that a mesh axis runs over, the one named last changes fastest.
Arguments:
- tokens: bfloat16 [2, 8192, 1152], P(None, 'fsdp'), may hold values from -6 to 6
- lengths: int32 [2, 8], replicated, may hold values from 1 to 2048, 8192 in all within a row
- query_weight: bfloat16 [1152, 1024], P('fsdp'), may hold values from -0.1875 to 0.1875
- key_weight: bfloat16 [1152, 256], P('fsdp'), may hold values from -0.1875 to 0.1875
- value_weight: bfloat16 [1152, 256], P('fsdp'), may hold values from -0.1875 to 0.1875
- output_weight: bfloat16 [1024, 1152], P('fsdp'), may hold values from -0.1875 to 0.1875
- gate_weight: bfloat16 [1152, 6912], P('fsdp'), may hold values from -0.1875 to 0.1875
- up_weight: bfloat16 [1152, 6912], P('fsdp'), may hold values from -0.1875 to 0.1875
- down_weight: bfloat16 [6912, 1152], P('fsdp'), may hold values from -0.078125 to 0.078125
- gains: bfloat16 [5120], P('fsdp'), may hold values from 0.099609375 to 1.8984375
- cotangent: bfloat16 [2, 8192, 1152], P(None, 'fsdp'), may hold values from -24 to 24
Outputs:
- activations: bfloat16 [2, 8192, 1152], P(None, 'fsdp')
- grad_tokens: float32 [2, 8192, 1152], P(None, 'fsdp')
- grad_query_weight: float32 [1152, 1024], P('fsdp')
- grad_key_weight: float32 [1152, 256], P('fsdp')
- grad_value_weight: float32 [1152, 256], P('fsdp')
- grad_output_weight: float32 [1024, 1152], P('fsdp')
- grad_gate_weight: float32 [1152, 6912], P('fsdp')
- grad_up_weight: float32 [1152, 6912], P('fsdp')
- grad_down_weight: float32 [6912, 1152], P('fsdp')
- grad_gains: float32 [5120], P('fsdp')
The draws below stay inside these ranges and needn't reach their ends.
Inputs may be any that keep to these rules, and one draw needn't show every extreme that they name: `lengths`: each row lists the sequences packed end to end into one micro-batch; a row sums to 8192 and its largest entry is 2048.
All inputs are finite; a program needn't handle non-finite values.
Results may differ from the reference program's by a relative error of at most 0.017.
Values may be sent and summed in bfloat16 or wider, within the bound.
No kernel may reach another device: no remote copies, remote signals or barrier semaphores. Data moves between devices by JAX's collectives and lax.ppermute only.
A program may use at most 384 MiB of HBM per device.

```python
import math
import jax
import jax.numpy as jnp
import numpy as np
from jax import lax

D = 1152
HEADS = 4
HD = 256
FF = 6912
WINDOW = 512
MB = 2
TOKENS = 8192
NSEQ = 8
LMAX = 2048
GAINS = 5120


def strengthened(array, stream_key, source, target, shards_of, factor):
    def block_of(dim):
        return (jnp.arange(array.shape[dim]) // (array.shape[dim] // shards_of)).reshape((-1,) + (1,) * (array.ndim - 1 - dim))

    one_side = jax.random.permutation(stream_key, shards_of)[block_of(target)]
    other_side = (block_of(target) + shards_of // 2) % shards_of
    return jnp.where((block_of(source) == one_side) | (block_of(source) == other_side), factor * array, array)


def block_levels(own_key, dims, pieces, least, high):
    loudness = 1.0
    for axis_at, blocks in pieces:
        steps = jax.random.uniform(jax.random.fold_in(jax.random.fold_in(own_key, 6), axis_at), (blocks,), jnp.float32, least / len(pieces), high / len(pieces))
        loudness = loudness * jnp.repeat(jnp.exp(steps), dims[axis_at] // blocks).reshape((-1,) + (1,) * (len(dims) - 1 - axis_at))
    return loudness


def length_profile(amount, total, limit, skew):
    weights = [(1 << 20) // math.isqrt(grade ** skew) + 1 for grade in range(2, amount + 1)]
    surplus, counts = total - limit - (amount - 1), [1] * (amount - 1)
    while surplus > 0:
        movable = [i for i in range(amount - 1) if counts[i] < limit]
        whole, remaining = sum([weights[i] for i in movable]), surplus
        for i in movable:
            extra = min(limit - counts[i], max(1, remaining * weights[i] // whole), surplus)
            counts[i] = counts[i] + extra
            surplus = surplus - extra
    return np.array([limit] + counts)


def ragged(own_key, amount, total, reach, skew):
    if amount == 2:
        one = jax.random.randint(own_key, (), max(1, total - reach), min(reach, total - 1) + 1)
        return jnp.stack([one, total - one])
    tallies = jnp.asarray(length_profile(amount, total, reach, skew), jnp.int32)
    couples = (amount - 1) // 2
    donor, taker = tallies[1:1 + 2 * couples:2], tallies[2:2 + 2 * couples:2]
    margin = jnp.minimum(donor - 1, reach - taker)
    shifted = jax.random.randint(jax.random.fold_in(own_key, 1), (couples,), 0, 1 << 20) % (margin + 1)
    tallies = tallies.at[1:1 + 2 * couples:2].set(donor - shifted).at[2:2 + 2 * couples:2].set(taker + shifted)
    return tallies[jax.random.permutation(jax.random.fold_in(own_key, 2), amount)]


def gaussian(own_key, shape, width, most, cuts=(), kind=jnp.bfloat16):
    values = width * jax.random.normal(own_key, shape, jnp.float32)
    if cuts:
        values = values * block_levels(own_key, shape, cuts, -0.22, 0.18)
    return jnp.clip(values, -most, most).astype(kind)


def heavy_noise(rng, extent, scale, reach, pieces, heavy, held_as=jnp.bfloat16):
    values = scale * jax.random.normal(rng, extent, jnp.float32)
    if pieces:
        values = values * block_levels(rng, extent, pieces, -0.22, 0.18)
    return jnp.clip(strengthened(values, jax.random.fold_in(rng, 3), *heavy), -reach, reach).astype(held_as)


def setup_inputs(seed: int = 0) -> dict:
    keys = jax.random.split(jax.random.key(seed), 12)
    tokens = gaussian(keys[0], (MB, TOKENS, D), 1.0, 6.0, ((1, 128),))
    lengths = jax.vmap(lambda own: ragged(own, NSEQ, TOKENS, LMAX, 2))(jax.random.split(keys[1], MB)).reshape((MB, NSEQ)).astype(jnp.int32)
    query_weight = gaussian(keys[2], (D, HEADS * HD), D ** -0.5, 0.1875, ((0, 128),))
    key_weight = gaussian(keys[3], (D, HD), D ** -0.5, 0.1875, ((0, 128),))
    value_weight = gaussian(keys[4], (D, HD), D ** -0.5, 0.1875, ((0, 128),))
    output_weight = gaussian(keys[5], (HEADS * HD, D), (HEADS * HD) ** -0.5, 0.1875, ((0, 128),))
    gate_weight = gaussian(keys[6], (D, FF), D ** -0.5, 0.1875, ((0, 128),))
    up_weight = gaussian(keys[7], (D, FF), D ** -0.5, 0.1875, ((0, 128),))
    down_weight = gaussian(keys[8], (FF, D), FF ** -0.5, 0.078125, ((0, 128),))
    gains = jnp.clip(1.0 + 0.18 * jax.random.normal(keys[9], (GAINS,), jnp.float32), 0.099609375, 1.8984375).astype(jnp.bfloat16)
    cotangent = heavy_noise(keys[10], (MB, TOKENS, D), 1.0, 24.0, ((1, 128),), (1, 2, 128, 5.5))
    return {"tokens": tokens, "lengths": lengths, "query_weight": query_weight, "key_weight": key_weight, "value_weight": value_weight, "output_weight": output_weight, "gate_weight": gate_weight, "up_weight": up_weight, "down_weight": down_weight, "gains": gains, "cotangent": cotangent}


EPS = 1e-06
ROPE_BASE = 10000.0
NEG = -1e+30
HIGHEST_PRECISION = lax.Precision.HIGHEST

@jax.custom_vjp
def low(v):
    return lax.optimization_barrier(v.astype(jnp.bfloat16)).astype(jnp.float32)

@jax.custom_vjp
def low_back(v):
    return v

def low_keep(v):
    return (low(v), None)

def low_pass(kept, grad):
    return (grad,)

def back_keep(v):
    return (v, None)

def back_low(kept, grad):
    return (low(grad),)
low.defvjp(low_keep, low_pass)
low_back.defvjp(back_keep, back_low)

def dense_product(operand, matrix):
    return jnp.dot(operand, matrix, precision=HIGHEST_PRECISION, preferred_element_type=jnp.float32)

def rms_norm(values, gain_vec):
    return values * lax.rsqrt(lax.optimization_barrier(jnp.mean(values * values, axis=-1, keepdims=True)) + EPS) * gain_vec

def rotate(values, cosine_table, sine_table):
    half_size = values.shape[-1] // 2
    turned = jnp.concatenate([-values[..., half_size:], values[..., :half_size]], axis=-1)
    return values * cosine_table + turned * sine_table

def rope_tables(position):
    frequency_index = jnp.arange(HD // 2, dtype=jnp.float32)
    inverse = ROPE_BASE ** (-2.0 * frequency_index / HD)
    angles = position.astype(jnp.float32)[..., None] * inverse
    angles = jnp.concatenate([angles, angles], axis=-1)
    return (jnp.cos(angles), jnp.sin(angles))

def layout(lengths, token_index):
    seq_ends = jnp.cumsum(lengths, axis=-1, dtype=jnp.int32)
    passed = seq_ends[..., None, :] <= token_index[..., :, None]
    seq_id = lax.optimization_barrier(jnp.sum(passed.astype(jnp.int32), axis=-1, dtype=jnp.int32))
    seq_start = lax.optimization_barrier(jnp.sum(jnp.where(passed, lengths[..., None, :], 0), axis=-1, dtype=jnp.int32))
    return (seq_id, token_index - seq_start)

def split_gains(flat_gains):
    return (flat_gains[0:D], flat_gains[D:2 * D], flat_gains[2 * D:3 * D], flat_gains[3 * D:4 * D], flat_gains[4 * D:4 * D + HD], flat_gains[4 * D + HD:4 * D + 2 * HD])

def windowed(queries, keys_rot, values_low, seq_id):
    stream_size = keys_rot.shape[0]
    blocks = stream_size // WINDOW
    lead_keys = jnp.concatenate([jnp.zeros((WINDOW, HD), jnp.float32), keys_rot])
    lead_values = jnp.concatenate([jnp.zeros((WINDOW, HD), jnp.float32), values_low])
    lead_seq = jnp.concatenate([jnp.full((WINDOW,), -1, jnp.int32), seq_id])
    score_scale = HD ** (-0.5)

    def one_block(number):
        first_row = number * WINDOW
        block_queries = lax.dynamic_slice_in_dim(queries, first_row, WINDOW, 0)
        block_keys = lax.dynamic_slice_in_dim(lead_keys, first_row, 2 * WINDOW, 0)
        block_values = lax.dynamic_slice_in_dim(lead_values, first_row, 2 * WINDOW, 0)
        seq_query = lax.dynamic_slice_in_dim(seq_id, first_row, WINDOW, 0)
        seq_key = lax.dynamic_slice_in_dim(lead_seq, first_row, 2 * WINDOW, 0)
        distance = jnp.arange(WINDOW, dtype=jnp.int32)[:, None] + WINDOW - jnp.arange(2 * WINDOW, dtype=jnp.int32)[None, :]
        allowed = (distance >= 0) & (distance < WINDOW) & (seq_query[:, None] == seq_key[None, :])
        scores = low_back(score_scale * jnp.einsum('qhd,kd->hqk', block_queries, block_keys, precision=HIGHEST_PRECISION))
        scores = jnp.where(allowed[None], scores, NEG)
        row_max = lax.optimization_barrier(jnp.max(scores, axis=-1, keepdims=True))
        weights = jnp.exp(scores - row_max)
        probs_f = weights / lax.optimization_barrier(jnp.sum(weights, axis=-1, keepdims=True))
        result = jnp.einsum('hqk,kd->qhd', low(probs_f), block_values, precision=HIGHEST_PRECISION)
        return low(low_back(result)).reshape(WINDOW, HEADS * HD)
    mixed_blocks = lax.map(jax.checkpoint(one_block), jnp.arange(blocks, dtype=jnp.int32))
    return mixed_blocks.reshape(stream_size, HEADS * HD)

def stream_forward(stream_inputs, lengths_row, weights):
    w_query, w_key, w_value, w_out, w_gate, w_up, w_down, flat_gains = weights
    gain_attn, gain_post_attn, gain_ffn, gain_post_ffn, gain_query, gain_key = split_gains(flat_gains)
    stream_size = stream_inputs.shape[0]
    seq_id, position = layout(lengths_row, jnp.arange(stream_size, dtype=jnp.int32))
    cosine_table, sine_table = rope_tables(position)
    attn_in = low(rms_norm(stream_inputs, gain_attn))
    query_raw = low_back(dense_product(attn_in, w_query)).reshape(stream_size, HEADS, HD)
    key_raw = low_back(dense_product(attn_in, w_key))
    values_low = low(low_back(dense_product(attn_in, w_value)))
    queries = low(rotate(rms_norm(query_raw, gain_query), cosine_table[:, None], sine_table[:, None]))
    keys_rot = low(rotate(rms_norm(key_raw, gain_key), cosine_table, sine_table))
    mixed_low = windowed(queries, keys_rot, values_low, seq_id)
    attn_out = low_back(dense_product(mixed_low, w_out))
    middle = stream_inputs + rms_norm(attn_out, gain_post_attn)
    ffn_in = low(rms_norm(middle, gain_ffn))
    gate_proj = low_back(dense_product(ffn_in, w_gate))
    up_proj = low_back(dense_product(ffn_in, w_up))
    hidden = low(jax.nn.gelu(gate_proj, approximate=True) * up_proj)
    down_proj = low_back(dense_product(hidden, w_down))
    return middle + rms_norm(down_proj, gain_post_ffn)

def reference(tokens, lengths, query_weight, key_weight, value_weight, output_weight, gate_weight, up_weight, down_weight, gains, cotangent):
    weights = tuple((matrix.astype(jnp.float32) for matrix in (query_weight, key_weight, value_weight, output_weight, gate_weight, up_weight, down_weight, gains)))
    inputs = tokens.astype(jnp.float32)

    def forward(stream_inputs, stream_weights):

        def one_stream(stream_pair):
            return stream_forward(stream_pair[0], stream_pair[1], stream_weights)
        return lax.map(jax.checkpoint(one_stream), (stream_inputs, lengths))
    result, pullback = jax.vjp(forward, inputs, weights)
    grad_inputs, gradients = pullback(cotangent.astype(jnp.float32))
    return (result.astype(jnp.bfloat16), grad_inputs, gradients[0], gradients[1], gradients[2], gradients[3], gradients[4], gradients[5], gradients[6], gradients[7])
```

```python
import jax
import jax.numpy as jnp
from jax import lax
from jax.sharding import Mesh, PartitionSpec as P

WINDOW = 512
EPS = 1e-06
ROPE_BASE = 10000.0
NEG = -1e30
ALL = ("y", "z", "x", "c")
RING = 4
ROWS = 128
BACK = 4
HALF = 768
OUT_SPLIT = 640
HID = 54
HID_PAD = 56
BF = jnp.bfloat16
F32 = jnp.float32


def rms_norm(values, gain_vec):
    return values * lax.rsqrt(jnp.mean(values * values, axis=-1, keepdims=True) + EPS) * gain_vec


def rotate(values, cosine_table, sine_table):
    half_size = values.shape[-1] // 2
    turned = jnp.concatenate([-values[..., half_size:], values[..., :half_size]], axis=-1)
    return values * cosine_table + turned * sine_table


def rope_tables(position, head_dim):
    frequency_index = jnp.arange(head_dim // 2, dtype=F32)
    inverse = ROPE_BASE ** (-2.0 * frequency_index / head_dim)
    angles = position.astype(F32)[..., None] * inverse
    cosine, sine = jnp.cos(angles), jnp.sin(angles)
    return (jnp.concatenate([cosine, cosine], -1), jnp.concatenate([sine, sine], -1))


def layout(lengths, token_index):
    seq_ends = jnp.cumsum(lengths, axis=-1, dtype=jnp.int32)
    passed = seq_ends[..., None, :] <= token_index[..., :, None]
    seq_id = jnp.sum(passed.astype(jnp.int32), axis=-1, dtype=jnp.int32)
    seq_start = jnp.sum(jnp.where(passed, lengths[..., None, :], 0), axis=-1, dtype=jnp.int32)
    return (seq_id, token_index - seq_start)


def gated_gelu(gate_proj, up_proj):
    return jax.nn.gelu(gate_proj, approximate=True) * up_proj


def product(operand, matrix):
    return jnp.dot(operand, matrix, preferred_element_type=F32)


def weight_grad(operand, grad_rows):
    return lax.dot_general(operand, grad_rows, (((0,), (0,)), ((), ())), preferred_element_type=F32)


def back_product(grad_rows, matrix):
    return lax.dot_general(grad_rows, matrix, (((1,), (1,)), ((), ())), preferred_element_type=F32)


def shift(value, axis, by):
    count = lax.axis_size(axis)
    return lax.ppermute(value, axis, [(i, (i + by) % count) for i in range(count)])


def swap(value):
    return shift(value, "c", 1)


def take(value, index, axis):
    return lax.dynamic_index_in_dim(value, index, axis, keepdims=False)


def gather(value, axis, at):
    me = lax.axis_index(axis)
    shape = value.shape[:at] + (RING,) + value.shape[at:]
    out = jnp.zeros(shape, value.dtype)
    for by in range(RING):
        block = shift(value, axis, by) if by else value
        out = lax.dynamic_update_index_in_dim(out, block, (me - by) % RING, at)
    return out


def exchange(value, axis, at):
    me = lax.axis_index(axis)
    out = jnp.zeros(value.shape, value.dtype)
    for by in range(RING):
        block = take(value, (me + by) % RING, at)
        block = shift(block, axis, by) if by else block
        out = lax.dynamic_update_index_in_dim(out, block, (me - by) % RING, at)
    return out


def reduce_to_owner(value, axis, at):
    me = lax.axis_index(axis)
    total = take(value, me, at).astype(F32)
    for by in range(1, RING):
        block = take(value, (me + by) % RING, at).astype(BF)
        total = total + shift(block, axis, by).astype(F32)
    return total


def plane_shift(value, by, late):
    pairs = []
    for index in range(128):
        y, z, rest, core = index // 32, index // 8 % 4, index % 8, index % 2
        if (core == 0) != late:
            y = (y + by) % RING
        else:
            z = (z + by) % RING
        pairs.append((index, (y * RING + z) * 8 + rest))
    return lax.ppermute(value, ALL, pairs)


def plane_gather(value, core, late):
    me = jnp.where((core == 0) != late, lax.axis_index("y"), lax.axis_index("z"))
    blocks = [value] + [plane_shift(value, by, late) for by in range(1, RING)]
    return in_order(blocks, me)


def in_order(blocks, me):
    out = jnp.zeros((RING,) + blocks[0].shape, blocks[0].dtype)
    for by, block in enumerate(blocks):
        out = lax.dynamic_update_index_in_dim(out, block, (me - by) % RING, 0)
    return out


def plane_blocks(value, core):
    y, z = lax.axis_index("y"), lax.axis_index("z")
    return [
        jnp.where(core == 0, take(value, (y + by) % RING, 0), take(value, (z + by) % RING, 1))
        for by in range(RING)
    ]


def plane_rest(total, core):
    me = jnp.where(core == 0, lax.axis_index("z"), lax.axis_index("y"))
    out = take(total, me, 0).astype(F32)
    for by in range(1, RING):
        part = take(total, (me + by) % RING, 0).astype(BF)
        out = out + plane_shift(part, by, True).astype(F32)
    return out


def add_up(blocks):
    return sum(block.astype(F32) for block in blocks)


def together(*values):
    return lax.optimization_barrier(values)


def fold_down(down, columns):
    count, _, width = down.shape
    rest = width - columns
    tail = down[:, :, columns:].reshape(count, HID_PAD // 8, 8, rest)
    tail = jnp.pad(tail, ((0, 0), (0, 2), (0, 0), (0, 0))).reshape(count, 3, 3, 8, rest)
    tail = tail.swapaxes(2, 3).reshape(count, 24, 3 * rest)
    tail = jnp.pad(tail, ((0, 0), (0, 0), (0, columns - 3 * rest)))
    return jnp.concatenate([down[:, :, :columns], tail], axis=1)


def unfold_down(folded, width):
    count, _, columns = folded.shape
    rest = width - columns
    tail = folded[:, HID_PAD:, : 3 * rest].reshape(count, 3, 8, 3, rest).swapaxes(2, 3)
    tail = tail.reshape(count, 72, rest)[:, :HID_PAD]
    return jnp.concatenate([folded[:, :HID_PAD], tail], axis=2)


def by_core(core, own, other):
    return jnp.where(core == 0, jnp.stack([own, other]), jnp.stack([other, own]))


def gather_tokens(rows):
    mine = jnp.concatenate([rows] + [shift(rows, "x", by) for by in range(1, RING)], axis=0)
    return jnp.concatenate([mine, swap(mine)], axis=0)


def scatter_tokens(partial):
    half = partial.shape[0] // 2
    mine = partial[:half] + swap(partial[half:].astype(BF)).astype(F32)
    blocks = mine.reshape(RING, half // RING, -1)
    total = blocks[0]
    for by in range(1, RING):
        total = total + shift(blocks[by].astype(BF), "x", -by).astype(F32)
    return total


def body(
    tokens,
    lengths,
    query_weight,
    key_weight,
    value_weight,
    output_weight,
    gate_weight,
    up_weight,
    down_weight,
    gains,
    cotangent,
):
    width = tokens.shape[2]
    head_dim = key_weight.shape[1]
    heads = query_weight.shape[1] // head_dim
    score_scale = head_dim ** (-0.5)
    y, z, x, core = (lax.axis_index(axis) for axis in ALL)
    group = y * RING + z
    chip = group * RING + x
    own_rows = query_weight.shape[0]
    out_rows = output_weight.shape[0]

    def to_core(value):
        own, other = take(value, core, 0), take(value, 1 - core, 0)
        return by_core(core, own, swap(other)).reshape(ROWS, width)

    def from_core(value):
        parts = value.reshape(2, ROWS // 2, width)
        return by_core(core, take(parts, core, 0), swap(take(parts, 1 - core, 0)))

    own_tokens = to_core(tokens)
    own_cotangent = to_core(cotangent)
    halo = [
        lax.ppermute(own_tokens, ALL, [(i, (i + 2 * by) % 128) for i in range(128)])
        for by in range(BACK, 0, -1)
    ]
    qkv_own = jnp.concatenate([query_weight, key_weight, value_weight], axis=1)
    gain_count = gains.shape[0]
    out_left = lax.dynamic_update_slice(
        jnp.pad(output_weight[:, :OUT_SPLIT], ((0, 0), (0, HALF - OUT_SPLIT))),
        gains[None],
        (0, OUT_SPLIT),
    )
    out_right = jnp.pad(output_weight[:, OUT_SPLIT:], ((0, 0), (0, HALF - width + OUT_SPLIT)))
    sides = jnp.stack(
        [
            jnp.concatenate([qkv_own[:, :HALF], out_left], axis=0),
            jnp.concatenate([qkv_own[:, HALF:], out_right], axis=0),
        ]
    )
    pair = by_core(core, take(sides, core, 0), swap(take(sides, 1 - core, 0)))
    blocks = gather(pair, "x", 0).reshape(8, own_rows + out_rows, HALF)
    qkv_rows = 8 * own_rows
    blocks = jnp.concatenate(
        [
            blocks[:, :own_rows].reshape(qkv_rows, HALF),
            blocks[:, own_rows:].reshape(8 * out_rows, HALF),
        ],
        axis=0,
    )
    hidden_size = 16 * HID_PAD

    def spread(matrix):
        parts = matrix.reshape(own_rows, 16, 8, HID).transpose(2, 0, 1, 3)
        return jnp.pad(parts, ((0, 0), (0, 0), (0, 0), (0, HID_PAD - HID))).reshape(
            8, own_rows, hidden_size
        )

    gate_up = jnp.concatenate([spread(gate_weight), spread(up_weight)], axis=-1)
    gate_up = gate_up.reshape(RING, 2, own_rows, 2 * hidden_size)
    gate_up = by_core(core, take(gate_up, core, 1), swap(take(gate_up, 1 - core, 1)))
    first = plane_gather(blocks, core, False)
    gate_up = exchange(gate_up, "x", 1)
    gate_up = gate_up.transpose(1, 0, 2, 3).reshape(qkv_rows, 2 * hidden_size)
    down_own = jnp.pad(down_weight, ((0, HID_PAD - HID), (0, 2 * hidden_size - width)))
    packed = jnp.concatenate([gate_up, down_own], axis=0)[None]
    first, packed, *halo = together(first, packed, *halo)
    packed = lax.all_gather(packed, ("y", "z"), axis=0, tiled=True)

    def both_sides(part):
        mine = plane_gather(part, core, True)
        theirs = swap(mine)
        left = jnp.where(core == 0, mine, theirs).swapaxes(0, 1)
        return left, jnp.where(core == 0, theirs, mine)

    left, right = both_sides(first[:, :qkv_rows])
    qkv_left, qkv_right = left.reshape(width, HALF), right.reshape(width, HALF)
    left, right = both_sides(first[:, qkv_rows:])
    out_left = left[..., :OUT_SPLIT].reshape(heads * head_dim, OUT_SPLIT)
    out_right = right[..., : width - OUT_SPLIT].reshape(heads * head_dim, width - OUT_SPLIT)
    flat_gains = left[..., OUT_SPLIT : OUT_SPLIT + gain_count]
    flat_gains = flat_gains.reshape(16, 8, out_rows, gain_count)[:, :, 0].reshape(-1).astype(F32)
    gain_attn, gain_post_attn, gain_ffn, gain_post_ffn = (
        flat_gains[n * width : (n + 1) * width] for n in range(4)
    )
    gain_query = flat_gains[4 * width : 4 * width + head_dim]
    gain_key = flat_gains[4 * width + head_dim :]

    own_lengths = take(lengths, core, 0)
    key_count = (BACK + 1) * ROWS
    key_index = (chip - BACK) * ROWS + jnp.arange(key_count, dtype=jnp.int32)
    key_seq, key_pos = layout(own_lengths, key_index)
    own_index, own_seq = key_index[-ROWS:], key_seq[-ROWS:]
    cosine_table, sine_table = rope_tables(key_pos, head_dim)
    own_cosine, own_sine = cosine_table[-ROWS:, None], sine_table[-ROWS:, None]
    inputs = own_tokens.astype(F32)
    attn_in, attn_pull = jax.vjp(rms_norm, inputs, gain_attn)
    halo_in = rms_norm(jnp.concatenate(halo, axis=0).astype(F32), gain_attn)
    window_low = jnp.concatenate([halo_in, attn_in], axis=0).astype(BF)
    attn_low = window_low[-ROWS:]
    third = heads * head_dim - HALF
    query_raw = jnp.concatenate(
        [product(attn_low, qkv_left), product(attn_low, qkv_right[:, :third])], axis=1
    ).reshape(ROWS, heads, head_dim)
    key_value_raw = product(window_low, qkv_right[:, third:])
    values_win = key_value_raw[:, head_dim:].astype(BF)

    def query_path(raw_vec, gain_vec):
        return rotate(rms_norm(raw_vec, gain_vec), own_cosine, own_sine)

    def key_path(raw_vec, gain_vec):
        return rotate(rms_norm(raw_vec, gain_vec), cosine_table, sine_table)

    queries, query_pull = jax.vjp(query_path, query_raw, gain_query)
    keys_rot, key_pull = jax.vjp(key_path, key_value_raw[:, :head_dim], gain_key)
    queries_low = queries.astype(BF)
    keys_win = keys_rot.astype(BF)
    distance = own_index[:, None] - key_index[None, :]
    allowed = (
        (key_index[None, :] >= 0)
        & (distance >= 0)
        & (distance < WINDOW)
        & (own_seq[:, None] == key_seq[None, :])
    )
    scores = jnp.einsum("qhd,kd->hqk", queries_low, keys_win, preferred_element_type=F32)
    scores = jnp.where(allowed[None], scores * score_scale, NEG)
    row_max = jnp.max(scores, axis=-1, keepdims=True)
    weights = jnp.exp(scores - row_max)
    probs = weights / jnp.sum(weights, axis=-1, keepdims=True)
    probs_low = probs.astype(BF)
    mixed = jnp.einsum("hqk,kd->qhd", probs_low, values_win, preferred_element_type=F32)
    mixed_low = mixed.astype(BF).reshape(ROWS, heads * head_dim)
    attn_out = jnp.concatenate(
        [product(mixed_low, out_left), product(mixed_low, out_right)], axis=1
    )
    post_attn, post_attn_pull = jax.vjp(rms_norm, attn_out, gain_post_attn)
    middle = inputs + post_attn
    ffn_in, ffn_pull = jax.vjp(rms_norm, middle, gain_ffn)

    w_gate_up = packed[:, :qkv_rows].reshape(width, 2 * hidden_size)
    w_down = packed[:, qkv_rows:, :width].reshape(hidden_size, width)
    ffn_low = gather_tokens(ffn_in.astype(BF))
    gate_up_proj = product(ffn_low, w_gate_up)
    hidden, hidden_pull = jax.vjp(
        gated_gelu, gate_up_proj[:, :hidden_size], gate_up_proj[:, hidden_size:]
    )
    hidden_low = hidden.astype(BF)
    down_proj = scatter_tokens(product(hidden_low, w_down))
    post_ffn, post_ffn_pull = jax.vjp(rms_norm, down_proj, gain_post_ffn)
    activations = from_core((middle + post_ffn).astype(BF))

    upstream = own_cotangent.astype(F32)
    grad_down_f, grad_gain_post_ffn = post_ffn_pull(upstream)
    grad_down_low = gather_tokens(grad_down_f.astype(BF))
    grad_gate_f, grad_up_f = hidden_pull(back_product(grad_down_low, w_down))
    grad_gate_up_low = jnp.concatenate([grad_gate_f, grad_up_f], axis=1).astype(BF)
    grad_ffn_in = scatter_tokens(back_product(grad_gate_up_low, w_gate_up))
    grad_w_down = weight_grad(hidden_low, grad_down_low).astype(BF)
    grad_w_gate_up = weight_grad(ffn_low, grad_gate_up_low).astype(BF)
    ffn_grads = jnp.concatenate(
        [
            grad_w_gate_up[:, :hidden_size].reshape(16, qkv_rows, hidden_size),
            grad_w_gate_up[:, hidden_size:].reshape(16, qkv_rows, hidden_size),
            fold_down(grad_w_down.reshape(16, HID_PAD, width), hidden_size),
        ],
        axis=1,
    ).reshape(RING, RING, -1, hidden_size)
    sums = plane_blocks(ffn_grads, core)
    grad_ffn_in, *sums = together(grad_ffn_in, *sums)
    sums = sums[:1] + [plane_shift(sums[by], by, False) for by in range(1, RING)]

    grad_middle_norm, grad_gain_ffn = ffn_pull(grad_ffn_in)
    grad_middle = upstream + grad_middle_norm
    grad_attn_f, grad_gain_post_attn = post_attn_pull(grad_middle)
    grad_attn_low = grad_attn_f.astype(BF)
    grad_mixed = back_product(grad_attn_low[:, :OUT_SPLIT], out_left) + back_product(
        grad_attn_low[:, OUT_SPLIT:], out_right
    )
    grad_mixed = grad_mixed.astype(BF).reshape(ROWS, heads, head_dim)
    grad_probs = jnp.einsum("qhd,kd->hqk", grad_mixed, values_win, preferred_element_type=F32)
    grad_values = jnp.einsum("hqk,qhd->kd", probs_low, grad_mixed, preferred_element_type=F32)
    grad_scores = probs * (grad_probs - jnp.sum(probs * grad_probs, axis=-1, keepdims=True))
    grad_scores_low = grad_scores.astype(BF)
    grad_queries = score_scale * jnp.einsum(
        "hqk,kd->qhd", grad_scores_low, keys_win, preferred_element_type=F32
    )
    grad_keys = score_scale * jnp.einsum(
        "hqk,qhd->kd", grad_scores_low, queries_low, preferred_element_type=F32
    )
    grad_query_raw, grad_gain_query = query_pull(grad_queries)
    grad_key_raw, grad_gain_key = key_pull(grad_keys)
    query_grad_low = grad_query_raw.astype(BF).reshape(ROWS, heads * head_dim)
    window_grad = jnp.concatenate([grad_key_raw, grad_values], axis=1)
    window_grad_low = window_grad.astype(BF)
    padded = jnp.concatenate([jnp.zeros((BACK * ROWS, heads * head_dim), BF), query_grad_low], axis=0)
    columns = (padded[:, :HALF], jnp.concatenate([padded[:, HALF:], window_grad_low], axis=1))
    out_columns = (
        jnp.pad(grad_attn_low[:, :OUT_SPLIT], ((0, 0), (0, HALF - OUT_SPLIT))),
        jnp.pad(grad_attn_low[:, OUT_SPLIT:], ((0, 0), (0, HALF - width + OUT_SPLIT))),
    )

    def side(is_left):
        qkv = weight_grad(window_low, jnp.where(is_left, *columns))
        out = weight_grad(mixed_low, jnp.where(is_left, *out_columns))
        factor = jnp.where(is_left, qkv_left, qkv_right).astype(F32)
        return qkv, out, jnp.sum(factor * qkv, axis=1)

    qkv_mine, out_mine, gain_mine = side(core == 0)
    qkv_theirs, out_theirs, gain_theirs = side(core == 1)
    grad_gain_attn = (gain_mine + gain_theirs) / gain_attn
    grad_gains = jnp.concatenate(
        [
            grad_gain_attn,
            grad_gain_post_attn,
            grad_gain_ffn,
            grad_gain_post_ffn,
            grad_gain_query,
            grad_gain_key,
        ]
    ).reshape(16, 8, gain_count)
    grad_gains = jnp.pad(grad_gains, ((0, 0), (0, 0), (0, HALF - gain_count)))

    def grid(array):
        return array.reshape(RING, RING, -1, HALF)

    theirs = jnp.concatenate(
        [grid(qkv_theirs), grid(out_theirs), grid(grad_gains)], axis=2
    ).astype(BF)
    mine = [grid(qkv_mine), grid(out_mine), grid(grad_gains)]
    mine, theirs, window_grad, window_grad_low, query_grad_low, grad_middle, sums = together(
        mine, theirs, window_grad, window_grad_low, query_grad_low, grad_middle, sums
    )
    other = swap(theirs)
    ffn_grads = plane_rest(add_up(sums), core)
    key_value_grad = window_grad[BACK * ROWS :]
    for by in range(1, BACK + 1):
        part = window_grad_low[(BACK - by) * ROWS : (BACK - by + 1) * ROWS]
        part = lax.ppermute(part, ALL, [(i, (i - 2 * by) % 128) for i in range(128)])
        key_value_grad = key_value_grad + part.astype(F32)

    def tokens_grad(key_value_grad):
        grad_right = jnp.concatenate([query_grad_low[:, HALF:], key_value_grad.astype(BF)], axis=1)
        grad_attn_in = back_product(query_grad_low[:, :HALF], qkv_left) + back_product(
            grad_right, qkv_right
        )
        return grad_middle + attn_pull(grad_attn_in)[0]

    start, parts = 0, []
    for part in mine:
        rows = part.shape[2]
        whole = part + other[:, :, start : start + rows].astype(F32)
        parts.append(plane_blocks(whole, core))
        start += rows
    sums = [jnp.concatenate([part[by] for part in parts], axis=1) for by in range(RING)]
    ffn_grads, key_value_grad, *sums = together(ffn_grads, key_value_grad, *sums)
    for by in range(1, RING):
        sums[by] = plane_shift(sums[by].astype(BF), by, False)
    back = ffn_grads[: 2 * qkv_rows].astype(BF).reshape(2, RING, 2, own_rows, hidden_size)
    back = exchange(back, "x", 1)
    back, grad_tokens, *sums = together(back, tokens_grad(key_value_grad), *sums)
    rows = plane_rest(add_up(sums), core)
    rows = jnp.concatenate(
        [
            rows[:qkv_rows].reshape(RING, 2, own_rows, HALF),
            rows[qkv_rows : qkv_rows + 8 * out_rows].reshape(RING, 2, out_rows, HALF),
            rows[qkv_rows + 8 * out_rows :].reshape(RING, 2, 1, HALF),
        ],
        axis=2,
    )
    pair = reduce_to_owner(rows, "x", 0)
    sides = by_core(core, take(pair, core, 0), swap(take(pair, 1 - core, 0)))
    grad_qkv = jnp.concatenate([sides[0, :own_rows], sides[1, :own_rows]], axis=1)
    grad_out = jnp.concatenate(
        [
            sides[0, own_rows : own_rows + out_rows, :OUT_SPLIT],
            sides[1, own_rows : own_rows + out_rows, : width - OUT_SPLIT],
        ],
        axis=1,
    )
    grad_gains = sides[0, own_rows + out_rows, :gain_count]

    back = by_core(core, take(back, core, 2), swap(take(back, 1 - core, 2)))
    back = back.reshape(2, 2, RING, own_rows, 16, HID_PAD)[..., :HID]
    back = back.transpose(1, 3, 4, 2, 0, 5).reshape(2, own_rows, 16 * 8 * HID).astype(F32)
    grad_w_down = unfold_down(ffn_grads[None, 2 * qkv_rows :], width)[0, :HID]
    return (
        activations,
        from_core(grad_tokens),
        grad_qkv[:, : heads * head_dim],
        grad_qkv[:, heads * head_dim : (heads + 1) * head_dim],
        grad_qkv[:, (heads + 1) * head_dim :],
        grad_out,
        back[0],
        back[1],
        grad_w_down,
        grad_gains,
    )


def solution(mesh):
    grid = Mesh(mesh.devices.reshape(RING, RING, RING, 2), ALL)
    row = P(ALL, None)
    token = P(None, ALL, None)
    in_specs = (token, P()) + (row,) * 7 + (P(ALL), token)
    out_specs = (token, token) + (row,) * 7 + (P(ALL),)
    return jax.shard_map(body, mesh=grid, in_specs=in_specs, out_specs=out_specs, check_vma=False)
```

```python
import jax
import jax.numpy as jnp
from jax import lax
from jax.experimental import pallas as pl
from jax.experimental.pallas import tpu as pltpu
from jax.sharding import Mesh, PartitionSpec as P

WINDOW = 512
EPS = 1e-06
ROPE_BASE = 10000.0
NEG = -1e30
ALL = ("y", "z", "x", "c")
RING = 4
ROWS = 128
BACK = 4
HALF = 768
OUT_SPLIT = 640
HID = 54
HID_PAD = 56
BF = jnp.bfloat16
F32 = jnp.float32


def rms_norm(values, gain_vec):
    return values * lax.rsqrt(jnp.mean(values * values, axis=-1, keepdims=True) + EPS) * gain_vec


def rotate(values, cosine_table, sine_table):
    half_size = values.shape[-1] // 2
    turned = jnp.concatenate([-values[..., half_size:], values[..., :half_size]], axis=-1)
    return values * cosine_table + turned * sine_table


def rope_tables(position, head_dim):
    frequency_index = jnp.arange(head_dim // 2, dtype=F32)
    inverse = ROPE_BASE ** (-2.0 * frequency_index / head_dim)
    angles = position.astype(F32)[..., None] * inverse
    cosine, sine = jnp.cos(angles), jnp.sin(angles)
    return (jnp.concatenate([cosine, cosine], -1), jnp.concatenate([sine, sine], -1))


def layout(lengths, token_index):
    seq_ends = jnp.cumsum(lengths, axis=-1, dtype=jnp.int32)
    passed = seq_ends[..., None, :] <= token_index[..., :, None]
    seq_id = jnp.sum(passed.astype(jnp.int32), axis=-1, dtype=jnp.int32)
    seq_start = jnp.sum(jnp.where(passed, lengths[..., None, :], 0), axis=-1, dtype=jnp.int32)
    return (seq_id, token_index - seq_start)


def gated_gelu(gate_proj, up_proj):
    return jax.nn.gelu(gate_proj, approximate=True) * up_proj


def product(operand, matrix):
    return jnp.dot(operand, matrix, preferred_element_type=F32)


def weight_grad(operand, grad_rows):
    return lax.dot_general(operand, grad_rows, (((0,), (0,)), ((), ())), preferred_element_type=F32)


def back_product(grad_rows, matrix):
    return lax.dot_general(grad_rows, matrix, (((1,), (1,)), ((), ())), preferred_element_type=F32)


def shift(value, axis, by):
    count = lax.axis_size(axis)
    return lax.ppermute(value, axis, [(i, (i + by) % count) for i in range(count)])


def swap(value):
    return shift(value, "c", 1)


def take(value, index, axis):
    return lax.dynamic_index_in_dim(value, index, axis, keepdims=False)


def gather(value, axis, at):
    me = lax.axis_index(axis)
    shape = value.shape[:at] + (RING,) + value.shape[at:]
    out = jnp.zeros(shape, value.dtype)
    for by in range(RING):
        block = shift(value, axis, by) if by else value
        out = lax.dynamic_update_index_in_dim(out, block, (me - by) % RING, at)
    return out


def exchange(value, axis, at):
    me = lax.axis_index(axis)
    out = jnp.zeros(value.shape, value.dtype)
    for by in range(RING):
        block = take(value, (me + by) % RING, at)
        block = shift(block, axis, by) if by else block
        out = lax.dynamic_update_index_in_dim(out, block, (me - by) % RING, at)
    return out


def reduce_to_owner(value, axis, at):
    me = lax.axis_index(axis)
    total = take(value, me, at).astype(F32)
    for by in range(1, RING):
        block = take(value, (me + by) % RING, at).astype(BF)
        total = total + shift(block, axis, by).astype(F32)
    return total


def plane_shift(value, by, late):
    pairs = []
    for index in range(128):
        y, z, rest, core = index // 32, index // 8 % 4, index % 8, index % 2
        if (core == 0) != late:
            y = (y + by) % RING
        else:
            z = (z + by) % RING
        pairs.append((index, (y * RING + z) * 8 + rest))
    return lax.ppermute(value, ALL, pairs)


def plane_gather(value, core, late):
    me = jnp.where((core == 0) != late, lax.axis_index("y"), lax.axis_index("z"))
    blocks = [value] + [plane_shift(value, by, late) for by in range(1, RING)]
    return in_order(blocks, me)


def in_order(blocks, me):
    out = jnp.zeros((RING,) + blocks[0].shape, blocks[0].dtype)
    for by, block in enumerate(blocks):
        out = lax.dynamic_update_index_in_dim(out, block, (me - by) % RING, 0)
    return out


def plane_blocks(value, core):
    y, z = lax.axis_index("y"), lax.axis_index("z")
    return [
        jnp.where(core == 0, take(value, (y + by) % RING, 0), take(value, (z + by) % RING, 1))
        for by in range(RING)
    ]


def plane_rest(total, core):
    me = jnp.where(core == 0, lax.axis_index("z"), lax.axis_index("y"))
    out = take(total, me, 0).astype(F32)
    for by in range(1, RING):
        part = take(total, (me + by) % RING, 0).astype(BF)
        out = out + plane_shift(part, by, True).astype(F32)
    return out


def shifted(blocks):
    return blocks[:1] + [plane_shift(blocks[by], by, False) for by in range(1, RING)]


def add_up(blocks):
    return sum(block.astype(F32) for block in blocks)


def together(*values):
    return lax.optimization_barrier(values)


def fold_down(down, columns):
    count, _, width = down.shape
    rest = width - columns
    tail = down[:, :, columns:].reshape(count, HID_PAD // 8, 8, rest)
    tail = jnp.pad(tail, ((0, 0), (0, 2), (0, 0), (0, 0))).reshape(count, 3, 3, 8, rest)
    tail = tail.swapaxes(2, 3).reshape(count, 24, 3 * rest)
    tail = jnp.pad(tail, ((0, 0), (0, 0), (0, columns - 3 * rest)))
    return jnp.concatenate([down[:, :, :columns], tail], axis=1)


def unfold_down(folded, width):
    count, _, columns = folded.shape
    rest = width - columns
    tail = folded[:, HID_PAD:, : 3 * rest].reshape(count, 3, 8, 3, rest).swapaxes(2, 3)
    tail = tail.reshape(count, 72, rest)[:, :HID_PAD]
    return jnp.concatenate([folded[:, :HID_PAD], tail], axis=2)


def by_core(core, own, other):
    return jnp.where(core == 0, jnp.stack([own, other]), jnp.stack([other, own]))


def gather_tokens(rows):
    mine = join([rows] + [shift(rows, "x", by) for by in range(1, RING)])
    return mine, swap(mine)


def scatter_tokens(mine, theirs):
    mine = mine + swap(theirs.astype(BF)).astype(F32)
    blocks = mine.reshape(RING, mine.shape[0] // RING, -1)
    total = blocks[0]
    for by in range(1, RING):
        total = total + shift(blocks[by].astype(BF), "x", -by).astype(F32)
    return total


def join_kernel(*refs):
    out = refs[-1]
    for n, block in enumerate(refs[:-1]):
        out[n * ROWS : (n + 1) * ROWS] = block[...]


def join(blocks):
    return pl.pallas_call(
        join_kernel,
        out_shape=jax.ShapeDtypeStruct((len(blocks) * ROWS,) + blocks[0].shape[1:], BF),
        compiler_params=pltpu.CompilerParams(vmem_limit_bytes=16 * 1024 * 1024),
        cost_estimate=pl.CostEstimate(flops=0, bytes_accessed=3 << 20, transcendentals=0),
    )(*blocks)


def matmul(left, right, contract):
    return lax.dot_general(left, right, ((contract[:1], contract[1:]), ((), ())), preferred_element_type=F32)


def attend_kernel(query_ref, bias_ref, *refs):
    blocks, (mixed_ref, probs_ref) = refs[:-2], refs[-2:]
    size = blocks[0].shape[1] // 2
    scale = size ** (-0.5)
    for head in range(query_ref.shape[1] // size):
        columns = slice(head * size, (head + 1) * size)
        query = query_ref[:, columns]
        scores = jnp.concatenate(
            [matmul(query, block[:, :size], (1, 1)) for block in blocks], axis=1
        )
        scores = scores * scale + bias_ref[...]
        weights = jnp.exp(scores - jnp.max(scores, axis=1, keepdims=True))
        probs = weights / jnp.sum(weights, axis=1, keepdims=True)
        probs_ref[head] = probs
        low = probs.astype(BF)
        mixed = sum(
            matmul(low[:, n * ROWS : (n + 1) * ROWS], block[:, size:], (1, 0))
            for n, block in enumerate(blocks)
        )
        mixed_ref[:, columns] = mixed.astype(BF)


def attend_back_kernel(query_ref, probs_ref, grad_ref, *refs):
    count = BACK + 1
    blocks, outs, query_out, total = refs[:count], refs[count:-2], refs[-2], refs[-1]
    size = blocks[0].shape[1] // 2
    scale = size ** (-0.5)
    for head in range(query_ref.shape[1] // size):
        columns = slice(head * size, (head + 1) * size)
        query, grad = query_ref[:, columns], grad_ref[:, columns]
        probs = probs_ref[head]
        grad_probs = jnp.concatenate(
            [matmul(grad, block[:, size:], (1, 1)) for block in blocks], axis=1
        )
        grad_scores = probs * (grad_probs - jnp.sum(probs * grad_probs, axis=1, keepdims=True))
        scores_low, probs_low = grad_scores.astype(BF), probs.astype(BF)
        grad_query = jnp.zeros((ROWS, size), F32)
        for n, block in enumerate(blocks):
            rows = slice(n * ROWS, (n + 1) * ROWS)
            grad_query += matmul(scores_low[:, rows], block[:, :size], (1, 0))
            grad_key = matmul(scores_low[:, rows], query, (0, 0)) * scale
            grad_value = matmul(probs_low[:, rows], grad, (0, 0))
            if head:
                grad_key += total[n, :, :size]
                grad_value += total[n, :, size:]
            total[n, :, :size] = grad_key
            total[n, :, size:] = grad_value
        query_out[:, columns] = grad_query * scale
    for n, out in enumerate(outs):
        out[...] = total[n].astype(out.dtype)


def attend(queries, bias, blocks):
    heads = queries.shape[1] // (blocks[0].shape[1] // 2)
    return pl.pallas_call(
        attend_kernel,
        out_shape=(
            jax.ShapeDtypeStruct(queries.shape, BF),
            jax.ShapeDtypeStruct((heads,) + bias.shape, F32),
        ),
        compiler_params=pltpu.CompilerParams(vmem_limit_bytes=32 * 1024 * 1024),
        cost_estimate=pl.CostEstimate(
            flops=4 * queries.size * bias.shape[1],
            bytes_accessed=4 << 20,
            transcendentals=heads * bias.size,
        ),
    )(queries, bias, *blocks)


def attend_back(queries, probs, grad, blocks):
    shape = blocks[0].shape
    *outs, query_out = pl.pallas_call(
        attend_back_kernel,
        out_shape=tuple(jax.ShapeDtypeStruct(shape, BF) for _ in range(BACK))
        + (jax.ShapeDtypeStruct(shape, F32), jax.ShapeDtypeStruct(queries.shape, F32)),
        scratch_shapes=[pltpu.VMEM((BACK + 1,) + shape, F32)],
        compiler_params=pltpu.CompilerParams(vmem_limit_bytes=32 * 1024 * 1024),
        cost_estimate=pl.CostEstimate(
            flops=8 * queries.size * probs.shape[2], bytes_accessed=6 << 20, transcendentals=0
        ),
    )(queries, probs, grad, *blocks)
    return outs, query_out


def pack_kernel(attn_ref, extra_ref, *refs):
    total = refs[-1]
    groups = 16
    rows = attn_ref.shape[1] // groups
    for columns, out in ((refs[0], refs[2]), (refs[1], refs[3])):
        for n in range(attn_ref.shape[1] // ROWS):
            part = slice(n * ROWS, (n + 1) * ROWS)
            total[part] = matmul(attn_ref[:, part], columns[...], (0, 0))
        for group in range(groups):
            block = jnp.concatenate(
                [total[group * rows : (group + 1) * rows], extra_ref[group]], axis=0
            )
            out[group] = block.astype(out.dtype)


def pack_out_kernel(mixed_ref, attn_ref, *refs):
    total = refs[-1]
    groups = 16
    rows, out_rows = attn_ref.shape[1] // groups, mixed_ref.shape[1] // groups
    sides = ((refs[0], refs[1], refs[4]), (refs[2], refs[3], refs[5]))
    for columns, out_columns, out in sides:
        for n in range(attn_ref.shape[1] // ROWS):
            part = slice(n * ROWS, (n + 1) * ROWS)
            total[part] = matmul(attn_ref[:, part], columns[...], (0, 0))
        blank = jnp.zeros((8, total.shape[1]), F32)
        for group in range(groups):
            block = jnp.concatenate([total[group * rows : (group + 1) * rows], blank], axis=0)
            out[group, out_rows:] = block.astype(out.dtype)
        for n in range(mixed_ref.shape[1] // ROWS):
            part = slice(n * ROWS, (n + 1) * ROWS)
            block = matmul(mixed_ref[:, part], out_columns[...], (0, 0)).astype(out.dtype)
            for k in range(ROWS // out_rows):
                group = n * (ROWS // out_rows) + k
                out[group, :out_rows] = block[k * out_rows : (k + 1) * out_rows]


def pack(kernel, rows, attn_low, other, *columns):
    columns_shape = columns[0].shape[1:]
    shape = (16, rows) + columns_shape
    operands = (attn_low, other) if kernel is pack_kernel else (other, attn_low)
    return pl.pallas_call(
        kernel,
        out_shape=(jax.ShapeDtypeStruct(shape, F32), jax.ShapeDtypeStruct(shape, BF)),
        scratch_shapes=[pltpu.VMEM((attn_low.shape[1],) + columns_shape, F32)],
        compiler_params=pltpu.CompilerParams(vmem_limit_bytes=40 * 1024 * 1024),
        cost_estimate=pl.CostEstimate(flops=1 << 30, bytes_accessed=12 << 20, transcendentals=0),
    )(*operands, *columns)


def cut_kernel(place_ref, mine_ref, other_ref, *outs):
    y, z, core = place_ref[0], place_ref[1], place_ref[2]
    for by, out in enumerate(outs):
        for rest in range(RING):
            group = jnp.where(
                core == 0, (y + by) % RING * RING + rest, rest * RING + (z + by) % RING
            )
            block = mine_ref[group] + other_ref[group].astype(F32)
            out[rest] = block.astype(out.dtype)


def cut(place, mine, other):
    shape = (RING,) + mine.shape[1:]
    vmem = pl.BlockSpec(memory_space=pltpu.VMEM)
    return pl.pallas_call(
        cut_kernel,
        in_specs=[pl.BlockSpec(memory_space=pltpu.SMEM), vmem, vmem],
        out_specs=(vmem,) * RING,
        out_shape=(jax.ShapeDtypeStruct(shape, F32),)
        + tuple(jax.ShapeDtypeStruct(shape, BF) for _ in range(1, RING)),
        compiler_params=pltpu.CompilerParams(vmem_limit_bytes=40 * 1024 * 1024),
        cost_estimate=pl.CostEstimate(flops=0, bytes_accessed=16 << 20, transcendentals=0),
    )(place, mine, other)


def body(
    tokens,
    lengths,
    query_weight,
    key_weight,
    value_weight,
    output_weight,
    gate_weight,
    up_weight,
    down_weight,
    gains,
    cotangent,
):
    width = tokens.shape[2]
    head_dim = key_weight.shape[1]
    heads = query_weight.shape[1] // head_dim
    y, z, x, core = (lax.axis_index(axis) for axis in ALL)
    group = y * RING + z
    chip = group * RING + x
    own_rows = query_weight.shape[0]
    out_rows = output_weight.shape[0]

    def to_core(value):
        own, other = take(value, core, 0), take(value, 1 - core, 0)
        return by_core(core, own, swap(other)).reshape(ROWS, width)

    def from_core(value):
        parts = value.reshape(2, ROWS // 2, width)
        return by_core(core, take(parts, core, 0), swap(take(parts, 1 - core, 0)))

    own_tokens = to_core(tokens)
    own_cotangent = to_core(cotangent)

    query_half = heads * head_dim // 2
    qkv_left = jnp.concatenate([key_weight, query_weight[:, :query_half]], axis=1)
    qkv_right = jnp.concatenate([value_weight, query_weight[:, query_half:]], axis=1)
    gain_count = gains.shape[0]
    own_parts = own_rows + 1 + out_rows
    gain_row = jnp.pad(gains[None], ((0, 0), (0, HALF - gain_count)))
    out_left = jnp.pad(output_weight[:, :OUT_SPLIT], ((0, 0), (0, HALF - OUT_SPLIT)))
    out_right = jnp.pad(output_weight[:, OUT_SPLIT:], ((0, 0), (0, HALF - width + OUT_SPLIT)))
    sides = jnp.stack(
        [
            jnp.concatenate([qkv_left, gain_row, out_left], axis=0),
            jnp.concatenate([qkv_right, gain_row, out_right], axis=0),
        ]
    )
    pair = by_core(core, take(sides, core, 0), swap(take(sides, 1 - core, 0)))
    qkv_rows = 8 * own_rows
    hidden_size = 16 * HID_PAD

    pair, gate_weight, up_weight = together(pair, gate_weight, up_weight)

    def spread(matrix):
        parts = matrix.reshape(own_rows, 16, 8, HID).transpose(2, 0, 1, 3)
        return jnp.pad(parts, ((0, 0), (0, 0), (0, 0), (0, HID_PAD - HID))).reshape(
            8, own_rows, hidden_size
        )

    blocks = gather(pair, "x", 0).reshape(8, own_parts, HALF)
    blocks = jnp.concatenate(
        [
            blocks[:, :own_rows].reshape(qkv_rows, HALF),
            blocks[:, own_rows],
            blocks[:, own_rows + 1 :].reshape(8 * out_rows, HALF),
        ],
        axis=0,
    )
    gate_up = jnp.concatenate([spread(gate_weight), spread(up_weight)], axis=-1)
    gate_up = gate_up.reshape(RING, 2, own_rows, 2 * hidden_size)
    gate_up = by_core(core, take(gate_up, core, 1), swap(take(gate_up, 1 - core, 1)))
    first = plane_gather(blocks, core, False)
    first, gate_up = together(first, exchange(gate_up, "x", 1))
    gate_up = gate_up.transpose(1, 0, 2, 3).reshape(qkv_rows, 2 * hidden_size)
    down_own = jnp.pad(down_weight, ((0, HID_PAD - HID), (0, 2 * hidden_size - width)))
    packed = jnp.concatenate([gate_up, down_own], axis=0)[None]
    packed = lax.all_gather(packed, ("y", "z"), axis=0, tiled=True)

    def both_sides(mine):
        theirs = swap(mine)
        left = jnp.where(core == 0, mine, theirs).swapaxes(0, 1)
        return left, jnp.where(core == 0, theirs, mine)

    early = qkv_rows + 8
    later = jnp.pad(first[:, :qkv_rows, head_dim:], ((0, 0), (0, 0), (0, OUT_SPLIT - query_half)))
    later = jnp.concatenate([later, first[:, early:, :OUT_SPLIT]], axis=1)
    mine, later = together(plane_gather(first[:, :early, :head_dim], core, True), later)
    left, right = both_sides(mine)
    w_key = left[:, :, :qkv_rows].reshape(width, head_dim)
    w_value = right[:, :, :qkv_rows].reshape(width, head_dim)
    flat_gains = left[:, :, qkv_rows:, :gain_count].reshape(-1).astype(F32)
    gain_attn, gain_post_attn, gain_ffn, gain_post_ffn = (
        flat_gains[n * width : (n + 1) * width] for n in range(4)
    )
    gain_query = flat_gains[4 * width : 4 * width + head_dim]
    gain_key = flat_gains[4 * width + head_dim :]

    own_lengths = take(lengths, core, 0)
    key_count = (BACK + 1) * ROWS
    key_index = (chip - BACK) * ROWS + jnp.arange(key_count, dtype=jnp.int32)
    key_seq, key_pos = layout(own_lengths, key_index)
    own_index, own_seq = key_index[-ROWS:], key_seq[-ROWS:]
    cosine_table, sine_table = rope_tables(key_pos[-ROWS:], head_dim)
    inputs = own_tokens.astype(F32)
    attn_in, attn_pull = jax.vjp(rms_norm, inputs, gain_attn)
    attn_low = attn_in.astype(BF)
    key_raw = product(attn_low, w_key)
    values_low = product(attn_low, w_value).astype(BF)

    def path(raw_vec, gain_vec):
        return rotate(rms_norm(raw_vec, gain_vec), cosine_table[:, None], sine_table[:, None])

    keys, key_pull = jax.vjp(path, key_raw[:, None], gain_key)
    key_value = jnp.concatenate([keys[:, 0].astype(BF), values_low], axis=1)
    key_value, attn_low = together(key_value, attn_low)
    window = [
        lax.ppermute(key_value, ALL, [(i, (i + 2 * by) % 128) for i in range(128)])
        for by in range(BACK, 0, -1)
    ]
    left, right = both_sides(plane_gather(later, core, True))
    query_left = left[:, :, :qkv_rows, :query_half].reshape(width, query_half)
    query_right = right[:, :, :qkv_rows, :query_half].reshape(width, query_half)
    out_left = left[:, :, qkv_rows:].reshape(heads * head_dim, OUT_SPLIT)
    out_right = right[:, :, qkv_rows:, : width - OUT_SPLIT].reshape(
        heads * head_dim, width - OUT_SPLIT
    )
    query_raw = jnp.concatenate(
        [product(attn_low, query_left), product(attn_low, query_right)], axis=1
    ).reshape(ROWS, heads, head_dim)
    queries, query_pull = jax.vjp(path, query_raw, gain_query)
    queries_low = queries.astype(BF).reshape(ROWS, heads * head_dim)
    queries_low, window = together(queries_low, window)
    window = window + [key_value]
    distance = own_index[:, None] - key_index[None, :]
    allowed = (
        (key_index[None, :] >= 0)
        & (distance >= 0)
        & (distance < WINDOW)
        & (own_seq[:, None] == key_seq[None, :])
    )
    bias = jnp.where(allowed, 0.0, NEG).astype(F32)
    mixed_low, probs = attend(queries_low, bias, window)
    attn_out = jnp.concatenate(
        [product(mixed_low, out_left), product(mixed_low, out_right)], axis=1
    )
    post_attn, post_attn_pull = jax.vjp(rms_norm, attn_out, gain_post_attn)
    middle = inputs + post_attn
    ffn_in, ffn_pull = jax.vjp(rms_norm, middle, gain_ffn)

    w_gate_up = packed[:, :qkv_rows].reshape(width, 2 * hidden_size)
    w_down = packed[:, qkv_rows:, :width].reshape(hidden_size, width)
    ffn_low = gather_tokens(ffn_in.astype(BF))

    def feed(rows):
        gate_up_proj = product(rows, w_gate_up)
        hidden, pull = jax.vjp(
            gated_gelu, gate_up_proj[:, :hidden_size], gate_up_proj[:, hidden_size:]
        )
        return hidden.astype(BF), pull

    hidden_low, hidden_pull = zip(*[feed(rows) for rows in ffn_low])
    down_proj = scatter_tokens(*[product(hidden, w_down) for hidden in hidden_low])
    post_ffn, post_ffn_pull = jax.vjp(rms_norm, down_proj, gain_post_ffn)
    activations = from_core((middle + post_ffn).astype(BF))

    upstream = own_cotangent.astype(F32)
    grad_down_f, grad_gain_post_ffn = post_ffn_pull(upstream)
    grad_down_low = gather_tokens(grad_down_f.astype(BF))
    grad_w_down = add_up(map(weight_grad, hidden_low, grad_down_low)).astype(BF)
    down_sums = fold_down(grad_w_down.reshape(16, HID_PAD, width), hidden_size)
    down_sums = plane_blocks(down_sums.reshape(RING, RING, -1, hidden_size), core)
    grad_down_low, down_sums = together(grad_down_low, down_sums)
    down_sums = shifted(down_sums)
    grad_gate_up_low = [
        jnp.concatenate(pull(back_product(rows, w_down)), axis=1).astype(BF)
        for pull, rows in zip(hidden_pull, grad_down_low)
    ]
    grad_ffn_in = scatter_tokens(*[back_product(rows, w_gate_up) for rows in grad_gate_up_low])
    grad_w_gate_up = add_up(map(weight_grad, ffn_low, grad_gate_up_low)).astype(BF)
    gate_up_sums = jnp.concatenate(
        [
            grad_w_gate_up[:, :hidden_size].reshape(16, qkv_rows, hidden_size),
            grad_w_gate_up[:, hidden_size:].reshape(16, qkv_rows, hidden_size),
        ],
        axis=1,
    ).reshape(RING, RING, -1, hidden_size)
    (gate_up_sums,) = together(gate_up_sums)
    gate_up_sums = plane_blocks(gate_up_sums, core)
    grad_ffn_in, gate_up_sums, down_sums = together(grad_ffn_in, gate_up_sums, down_sums)
    gate_up_sums = shifted(gate_up_sums)
    grad_middle_norm, grad_gain_ffn = ffn_pull(grad_ffn_in)
    grad_middle = upstream + grad_middle_norm
    grad_attn_f, grad_gain_post_attn = post_attn_pull(grad_middle)
    grad_attn_low = grad_attn_f.astype(BF)
    grad_mixed = back_product(grad_attn_low[:, :OUT_SPLIT], out_left) + back_product(
        grad_attn_low[:, OUT_SPLIT:], out_right
    )
    (*parts, key_value_grad), grad_queries = attend_back(
        queries_low, probs, grad_mixed.astype(BF), window
    )
    for by in range(1, BACK + 1):
        part = parts[BACK - by]
        part = lax.ppermute(part, ALL, [(i, (i - 2 * by) % 128) for i in range(128)])
        key_value_grad = key_value_grad + part.astype(F32)
    grad_queries = grad_queries.reshape(ROWS, heads, head_dim)
    grad_query_raw, grad_gain_query = query_pull(grad_queries)
    query_grad_low = grad_query_raw.astype(BF).reshape(ROWS, heads * head_dim)
    place = jnp.stack([y, z, core])

    def mine_theirs(left, right):
        return jnp.where(core == 0, left, right), jnp.where(core == 0, right, left)

    sides = mine_theirs(query_grad_low[:, :query_half], query_grad_low[:, query_half:])
    sides = [jnp.pad(side, ((0, 0), (0, OUT_SPLIT - query_half))) for side in sides]
    out_sides = mine_theirs(
        grad_attn_low[:, :OUT_SPLIT],
        jnp.pad(grad_attn_low[:, OUT_SPLIT:], ((0, 0), (0, 2 * OUT_SPLIT - width))),
    )
    mine, theirs = pack(
        pack_out_kernel,
        qkv_rows + 8 * out_rows + 8,
        attn_low,
        mixed_low,
        *(side for pair in zip(sides, out_sides) for side in pair),
    )
    sums = list(cut(place, mine, swap(theirs)))
    key_value_grad, gate_up_sums, sums = together(key_value_grad, gate_up_sums, sums)
    sums = shifted(sums)
    grad_key_raw, grad_gain_key = key_pull(key_value_grad[:, None, :head_dim])
    key_low = grad_key_raw[:, 0].astype(BF)
    value_low = key_value_grad[:, head_dim:].astype(BF)
    grad_attn_in = (
        back_product(query_grad_low[:, :query_half], query_left)
        + back_product(query_grad_low[:, query_half:], query_right)
        + back_product(key_low, w_key)
        + back_product(value_low, w_value)
    )
    grad_inputs_norm, grad_gain_attn = attn_pull(grad_attn_in)
    grad_tokens = grad_middle + grad_inputs_norm
    grad_gains = jnp.concatenate(
        [
            grad_gain_attn,
            grad_gain_post_attn,
            grad_gain_ffn,
            grad_gain_post_ffn,
            grad_gain_query,
            grad_gain_key,
        ]
    ).reshape(16, 8, gain_count)
    grad_gains = jnp.pad(grad_gains, ((0, 0), (0, 0), (0, head_dim - gain_count)))
    mine, theirs = pack(
        pack_kernel, qkv_rows + 8, attn_low, grad_gains, *mine_theirs(key_low, value_low)
    )
    late_sums = list(cut(place, mine, swap(theirs)))
    sums, late_sums, grad_tokens = together(sums, late_sums, grad_tokens)
    late_sums = shifted(late_sums)
    ffn_grads = jnp.concatenate([add_up(gate_up_sums), add_up(down_sums)], axis=1)
    ffn_grads = plane_rest(ffn_grads, core)
    late_sum = jnp.pad(add_up(late_sums), ((0, 0), (0, 0), (0, OUT_SPLIT - head_dim)))
    total = jnp.concatenate([add_up(sums)[:, :-8], late_sum], axis=1)
    total, ffn_grads = together(total, ffn_grads)

    back = ffn_grads[: 2 * qkv_rows].astype(BF).reshape(2, RING, 2, own_rows, hidden_size)
    back = exchange(back, "x", 1)
    back = by_core(core, take(back, core, 2), swap(take(back, 1 - core, 2)))
    back = back.reshape(2, 2, RING, own_rows, 16, HID_PAD)[..., :HID]
    back = back.transpose(1, 3, 4, 2, 0, 5).reshape(2, own_rows, 16 * 8 * HID).astype(F32)
    grad_w_down = unfold_down(ffn_grads[None, 2 * qkv_rows :], width)[0, :HID]
    rows = plane_rest(total, core)
    bounds = [0, 8 * out_rows]
    bounds += [bounds[1] + qkv_rows, bounds[1] + 2 * qkv_rows, bounds[1] + 2 * qkv_rows + 8]
    rows = jnp.concatenate(
        [
            rows[low:high].reshape(RING, 2, -1, OUT_SPLIT)
            for low, high in zip(bounds[:-1], bounds[1:])
        ],
        axis=2,
    )
    pair, back, grad_w_down = together(reduce_to_owner(rows, "x", 0), back, grad_w_down)
    sides = by_core(core, take(pair, core, 0), swap(take(pair, 1 - core, 0)))
    kinds = [0, out_rows, out_rows + own_rows, out_rows + 2 * own_rows]
    grad_query = jnp.concatenate(
        [sides[n, kinds[1] : kinds[2], :query_half] for n in range(2)], axis=1
    )
    grad_out = jnp.concatenate(
        [sides[0, : kinds[1]], sides[1, : kinds[1], : width - OUT_SPLIT]], axis=1
    )
    grad_key, grad_value = (sides[n, kinds[2] : kinds[3], :head_dim] for n in range(2))
    grad_gains = sides[0, kinds[3], :gain_count]
    return (
        activations,
        from_core(grad_tokens),
        grad_query,
        grad_key,
        grad_value,
        grad_out,
        back[0],
        back[1],
        grad_w_down,
        grad_gains,
    )


def solution(mesh):
    grid = Mesh(mesh.devices.reshape(RING, RING, RING, 2), ALL)
    row = P(ALL, None)
    token = P(None, ALL, None)
    in_specs = (token, P()) + (row,) * 7 + (P(ALL), token)
    out_specs = (token, token) + (row,) * 7 + (P(ALL),)
    return jax.shard_map(body, mesh=grid, in_specs=in_specs, out_specs=out_specs, check_vma=False)
```

```python
import jax
import jax.numpy as jnp
from jax import lax
from jax.experimental import pallas as pl
from jax.experimental.pallas import tpu as pltpu
from jax.sharding import Mesh, PartitionSpec as P

WINDOW = 512
EPS = 1e-06
ROPE_BASE = 10000.0
NEG = -1e30
ALL = ("y", "z", "x", "c")
RING = 4
ROWS = 128
BACK = 4
HALF = 768
OUT_SPLIT = 640
HID = 54
HID_PAD = 56
BF = jnp.bfloat16
F32 = jnp.float32


def rms_norm(values, gain_vec):
    return values * lax.rsqrt(jnp.mean(values * values, axis=-1, keepdims=True) + EPS) * gain_vec


def rotate(values, cosine_table, sine_table):
    half_size = values.shape[-1] // 2
    turned = jnp.concatenate([-values[..., half_size:], values[..., :half_size]], axis=-1)
    return values * cosine_table + turned * sine_table


def rope_tables(position, head_dim):
    frequency_index = jnp.arange(head_dim // 2, dtype=F32)
    inverse = ROPE_BASE ** (-2.0 * frequency_index / head_dim)
    angles = position.astype(F32)[..., None] * inverse
    cosine, sine = jnp.cos(angles), jnp.sin(angles)
    return (jnp.concatenate([cosine, cosine], -1), jnp.concatenate([sine, sine], -1))


def layout(lengths, token_index):
    seq_ends = jnp.cumsum(lengths, axis=-1, dtype=jnp.int32)
    passed = seq_ends[..., None, :] <= token_index[..., :, None]
    seq_id = jnp.sum(passed.astype(jnp.int32), axis=-1, dtype=jnp.int32)
    seq_start = jnp.sum(jnp.where(passed, lengths[..., None, :], 0), axis=-1, dtype=jnp.int32)
    return (seq_id, token_index - seq_start)


def gated_gelu(gate_proj, up_proj):
    return jax.nn.gelu(gate_proj, approximate=True) * up_proj


def product(operand, matrix):
    return jnp.dot(operand, matrix, preferred_element_type=F32)


def weight_grad(operand, grad_rows):
    return lax.dot_general(operand, grad_rows, (((0,), (0,)), ((), ())), preferred_element_type=F32)


def back_product(grad_rows, matrix):
    return lax.dot_general(grad_rows, matrix, (((1,), (1,)), ((), ())), preferred_element_type=F32)


def shift(value, axis, by):
    count = lax.axis_size(axis)
    return lax.ppermute(value, axis, [(i, (i + by) % count) for i in range(count)])


def swap(value):
    return shift(value, "c", 1)


def take(value, index, axis):
    return lax.dynamic_index_in_dim(value, index, axis, keepdims=False)


def gather(value, axis, at):
    me = lax.axis_index(axis)
    shape = value.shape[:at] + (RING,) + value.shape[at:]
    out = jnp.zeros(shape, value.dtype)
    for by in range(RING):
        block = shift(value, axis, by) if by else value
        out = lax.dynamic_update_index_in_dim(out, block, (me - by) % RING, at)
    return out


def exchange(value, axis, at):
    me = lax.axis_index(axis)
    out = jnp.zeros(value.shape, value.dtype)
    for by in range(RING):
        block = take(value, (me + by) % RING, at)
        block = shift(block, axis, by) if by else block
        out = lax.dynamic_update_index_in_dim(out, block, (me - by) % RING, at)
    return out


def reduce_to_owner(value, axis, at):
    me = lax.axis_index(axis)
    total = take(value, me, at).astype(F32)
    for by in range(1, RING):
        block = take(value, (me + by) % RING, at).astype(BF)
        total = total + shift(block, axis, by).astype(F32)
    return total


def plane_shift(value, by, late):
    pairs = []
    for index in range(128):
        y, z, rest, core = index // 32, index // 8 % 4, index % 8, index % 2
        if (core == 0) != late:
            y = (y + by) % RING
        else:
            z = (z + by) % RING
        pairs.append((index, (y * RING + z) * 8 + rest))
    return lax.ppermute(value, ALL, pairs)


def plane_gather(value, core, late):
    me = jnp.where((core == 0) != late, lax.axis_index("y"), lax.axis_index("z"))
    blocks = [value] + [plane_shift(value, by, late) for by in range(1, RING)]
    return in_order(blocks, me)


def in_order(blocks, me):
    out = jnp.zeros((RING,) + blocks[0].shape, blocks[0].dtype)
    for by, block in enumerate(blocks):
        out = lax.dynamic_update_index_in_dim(out, block, (me - by) % RING, 0)
    return out


def plane_blocks(value, core):
    y, z = lax.axis_index("y"), lax.axis_index("z")
    return [
        jnp.where(core == 0, take(value, (y + by) % RING, 0), take(value, (z + by) % RING, 1))
        for by in range(RING)
    ]


def plane_rest(total, core):
    me = jnp.where(core == 0, lax.axis_index("z"), lax.axis_index("y"))
    out = take(total, me, 0).astype(F32)
    for by in range(1, RING):
        part = take(total, (me + by) % RING, 0).astype(BF)
        out = out + plane_shift(part, by, True).astype(F32)
    return out


def shifted(blocks):
    return blocks[:1] + [plane_shift(blocks[by], by, False) for by in range(1, RING)]


def add_up(blocks):
    return sum(block.astype(F32) for block in blocks)


def together(*values):
    return lax.optimization_barrier(values)


def fold_down(down, columns):
    count, _, width = down.shape
    rest = width - columns
    tail = down[:, :, columns:].reshape(count, HID_PAD // 8, 8, rest)
    tail = jnp.pad(tail, ((0, 0), (0, 2), (0, 0), (0, 0))).reshape(count, 3, 3, 8, rest)
    tail = tail.swapaxes(2, 3).reshape(count, 24, 3 * rest)
    tail = jnp.pad(tail, ((0, 0), (0, 0), (0, columns - 3 * rest)))
    return jnp.concatenate([down[:, :, :columns], tail], axis=1)


def unfold_down(folded, width):
    count, _, columns = folded.shape
    rest = width - columns
    tail = folded[:, HID_PAD:, : 3 * rest].reshape(count, 3, 8, 3, rest).swapaxes(2, 3)
    tail = tail.reshape(count, 72, rest)[:, :HID_PAD]
    return jnp.concatenate([folded[:, :HID_PAD], tail], axis=2)


def by_core(core, own, other):
    return jnp.where(core == 0, jnp.stack([own, other]), jnp.stack([other, own]))


def gather_tokens(rows):
    mine = join([rows] + [shift(rows, "x", by) for by in range(1, RING)])
    return mine, swap(mine)


def scatter_tokens(mine, theirs):
    mine = mine + swap(theirs.astype(BF)).astype(F32)
    blocks = mine.reshape(RING, mine.shape[0] // RING, -1)
    total = blocks[0]
    for by in range(1, RING):
        total = total + shift(blocks[by].astype(BF), "x", -by).astype(F32)
    return total


def join_kernel(*refs):
    out = refs[-1]
    for n, block in enumerate(refs[:-1]):
        out[n * ROWS : (n + 1) * ROWS] = block[...]


def join(blocks):
    return pl.pallas_call(
        join_kernel,
        out_shape=jax.ShapeDtypeStruct((len(blocks) * ROWS,) + blocks[0].shape[1:], BF),
        compiler_params=pltpu.CompilerParams(vmem_limit_bytes=16 * 1024 * 1024),
        cost_estimate=pl.CostEstimate(flops=0, bytes_accessed=3 << 20, transcendentals=0),
    )(*blocks)


def matmul(left, right, contract):
    return lax.dot_general(left, right, ((contract[:1], contract[1:]), ((), ())), preferred_element_type=F32)


def attend_kernel(query_ref, bias_ref, *refs):
    blocks, (mixed_ref, probs_ref) = refs[:-2], refs[-2:]
    size = blocks[0].shape[1] // 2
    scale = size ** (-0.5)
    for head in range(query_ref.shape[1] // size):
        columns = slice(head * size, (head + 1) * size)
        query = query_ref[:, columns]
        scores = jnp.concatenate(
            [matmul(query, block[:, :size], (1, 1)) for block in blocks], axis=1
        )
        scores = scores * scale + bias_ref[...]
        weights = jnp.exp(scores - jnp.max(scores, axis=1, keepdims=True))
        probs = weights / jnp.sum(weights, axis=1, keepdims=True)
        probs_ref[head] = probs
        low = probs.astype(BF)
        mixed = sum(
            matmul(low[:, n * ROWS : (n + 1) * ROWS], block[:, size:], (1, 0))
            for n, block in enumerate(blocks)
        )
        mixed_ref[:, columns] = mixed.astype(BF)


def attend_back_kernel(query_ref, probs_ref, grad_ref, *refs):
    count = BACK + 1
    blocks, outs, query_out, total = refs[:count], refs[count:-2], refs[-2], refs[-1]
    size = blocks[0].shape[1] // 2
    scale = size ** (-0.5)
    for head in range(query_ref.shape[1] // size):
        columns = slice(head * size, (head + 1) * size)
        query, grad = query_ref[:, columns], grad_ref[:, columns]
        probs = probs_ref[head]
        grad_probs = jnp.concatenate(
            [matmul(grad, block[:, size:], (1, 1)) for block in blocks], axis=1
        )
        grad_scores = probs * (grad_probs - jnp.sum(probs * grad_probs, axis=1, keepdims=True))
        scores_low, probs_low = grad_scores.astype(BF), probs.astype(BF)
        grad_query = jnp.zeros((ROWS, size), F32)
        for n, block in enumerate(blocks):
            rows = slice(n * ROWS, (n + 1) * ROWS)
            grad_query += matmul(scores_low[:, rows], block[:, :size], (1, 0))
            grad_key = matmul(scores_low[:, rows], query, (0, 0)) * scale
            grad_value = matmul(probs_low[:, rows], grad, (0, 0))
            if head:
                grad_key += total[n, :, :size]
                grad_value += total[n, :, size:]
            total[n, :, :size] = grad_key
            total[n, :, size:] = grad_value
        query_out[:, columns] = grad_query * scale
    for n, out in enumerate(outs):
        out[...] = total[n].astype(out.dtype)


def attend(queries, bias, blocks):
    heads = queries.shape[1] // (blocks[0].shape[1] // 2)
    return pl.pallas_call(
        attend_kernel,
        out_shape=(
            jax.ShapeDtypeStruct(queries.shape, BF),
            jax.ShapeDtypeStruct((heads,) + bias.shape, F32),
        ),
        compiler_params=pltpu.CompilerParams(vmem_limit_bytes=32 * 1024 * 1024),
        cost_estimate=pl.CostEstimate(
            flops=4 * queries.size * bias.shape[1],
            bytes_accessed=4 << 20,
            transcendentals=heads * bias.size,
        ),
    )(queries, bias, *blocks)


def attend_back(queries, probs, grad, blocks):
    shape = blocks[0].shape
    *outs, query_out = pl.pallas_call(
        attend_back_kernel,
        out_shape=tuple(jax.ShapeDtypeStruct(shape, BF) for _ in range(BACK))
        + (jax.ShapeDtypeStruct(shape, F32), jax.ShapeDtypeStruct(queries.shape, F32)),
        scratch_shapes=[pltpu.VMEM((BACK + 1,) + shape, F32)],
        compiler_params=pltpu.CompilerParams(vmem_limit_bytes=32 * 1024 * 1024),
        cost_estimate=pl.CostEstimate(flops=1 << 10, bytes_accessed=1 << 10, transcendentals=0),
    )(queries, probs, grad, *blocks)
    return outs, query_out


def pack_kernel(attn_ref, extra_ref, *refs):
    total = refs[-1]
    groups = 16
    rows = attn_ref.shape[1] // groups
    for columns, out in ((refs[0], refs[2]), (refs[1], refs[3])):
        for n in range(attn_ref.shape[1] // ROWS):
            part = slice(n * ROWS, (n + 1) * ROWS)
            total[part] = matmul(attn_ref[:, part], columns[...], (0, 0))
        for group in range(groups):
            block = jnp.concatenate(
                [total[group * rows : (group + 1) * rows], extra_ref[group]], axis=0
            )
            out[group] = block.astype(out.dtype)


def pack_out_kernel(mixed_ref, attn_ref, *refs):
    total = refs[-1]
    groups = 16
    rows, out_rows = attn_ref.shape[1] // groups, mixed_ref.shape[1] // groups
    sides = ((refs[0], refs[1], refs[4]), (refs[2], refs[3], refs[5]))
    for columns, out_columns, out in sides:
        for n in range(attn_ref.shape[1] // ROWS):
            part = slice(n * ROWS, (n + 1) * ROWS)
            total[part] = matmul(attn_ref[:, part], columns[...], (0, 0))
        blank = jnp.zeros((8, total.shape[1]), F32)
        for group in range(groups):
            block = jnp.concatenate([total[group * rows : (group + 1) * rows], blank], axis=0)
            out[group, out_rows:] = block.astype(out.dtype)
        for n in range(mixed_ref.shape[1] // ROWS):
            part = slice(n * ROWS, (n + 1) * ROWS)
            block = matmul(mixed_ref[:, part], out_columns[...], (0, 0)).astype(out.dtype)
            for k in range(ROWS // out_rows):
                group = n * (ROWS // out_rows) + k
                out[group, :out_rows] = block[k * out_rows : (k + 1) * out_rows]


def pack(kernel, rows, attn_low, other, *columns):
    columns_shape = columns[0].shape[1:]
    shape = (16, rows) + columns_shape
    operands = (attn_low, other) if kernel is pack_kernel else (other, attn_low)
    return pl.pallas_call(
        kernel,
        out_shape=(jax.ShapeDtypeStruct(shape, F32), jax.ShapeDtypeStruct(shape, BF)),
        scratch_shapes=[pltpu.VMEM((attn_low.shape[1],) + columns_shape, F32)],
        compiler_params=pltpu.CompilerParams(vmem_limit_bytes=40 * 1024 * 1024),
        cost_estimate=pl.CostEstimate(flops=1 << 10, bytes_accessed=1 << 10, transcendentals=0),
    )(*operands, *columns)


def cut_kernel(place_ref, mine_ref, other_ref, *outs):
    y, z, core = place_ref[0], place_ref[1], place_ref[2]
    for by, out in enumerate(outs):
        for rest in range(RING):
            group = jnp.where(
                core == 0, (y + by) % RING * RING + rest, rest * RING + (z + by) % RING
            )
            block = mine_ref[group] + other_ref[group].astype(F32)
            out[rest] = block.astype(out.dtype)


def cut(place, mine, other):
    shape = (RING,) + mine.shape[1:]
    vmem = pl.BlockSpec(memory_space=pltpu.VMEM)
    return pl.pallas_call(
        cut_kernel,
        in_specs=[pl.BlockSpec(memory_space=pltpu.SMEM), vmem, vmem],
        out_specs=(vmem,) * RING,
        out_shape=(jax.ShapeDtypeStruct(shape, F32),)
        + tuple(jax.ShapeDtypeStruct(shape, BF) for _ in range(1, RING)),
        compiler_params=pltpu.CompilerParams(vmem_limit_bytes=40 * 1024 * 1024),
        cost_estimate=pl.CostEstimate(flops=1 << 10, bytes_accessed=1 << 10, transcendentals=0),
    )(place, mine, other)


def body(
    tokens,
    lengths,
    query_weight,
    key_weight,
    value_weight,
    output_weight,
    gate_weight,
    up_weight,
    down_weight,
    gains,
    cotangent,
):
    width = tokens.shape[2]
    head_dim = key_weight.shape[1]
    heads = query_weight.shape[1] // head_dim
    y, z, x, core = (lax.axis_index(axis) for axis in ALL)
    group = y * RING + z
    chip = group * RING + x
    own_rows = query_weight.shape[0]
    out_rows = output_weight.shape[0]

    def to_core(value):
        own, other = take(value, core, 0), take(value, 1 - core, 0)
        return by_core(core, own, swap(other)).reshape(ROWS, width)

    def from_core(value):
        parts = value.reshape(2, ROWS // 2, width)
        return by_core(core, take(parts, core, 0), swap(take(parts, 1 - core, 0)))

    own_tokens = to_core(tokens)
    own_cotangent = to_core(cotangent)

    query_half = heads * head_dim // 2
    qkv_left = jnp.concatenate([key_weight, query_weight[:, :query_half]], axis=1)
    qkv_right = jnp.concatenate([value_weight, query_weight[:, query_half:]], axis=1)
    gain_count = gains.shape[0]
    own_parts = own_rows + 1 + out_rows
    gain_row = jnp.pad(gains[None], ((0, 0), (0, HALF - gain_count)))
    out_left = jnp.pad(output_weight[:, :OUT_SPLIT], ((0, 0), (0, HALF - OUT_SPLIT)))
    out_right = jnp.pad(output_weight[:, OUT_SPLIT:], ((0, 0), (0, HALF - width + OUT_SPLIT)))
    sides = jnp.stack(
        [
            jnp.concatenate([qkv_left, gain_row, out_left], axis=0),
            jnp.concatenate([qkv_right, gain_row, out_right], axis=0),
        ]
    )
    pair = by_core(core, take(sides, core, 0), swap(take(sides, 1 - core, 0)))
    qkv_rows = 8 * own_rows
    hidden_size = 16 * HID_PAD

    pair, gate_weight, up_weight = together(pair, gate_weight, up_weight)

    def spread(matrix):
        parts = matrix.reshape(own_rows, 16, 8, HID).transpose(2, 0, 1, 3)
        return jnp.pad(parts, ((0, 0), (0, 0), (0, 0), (0, HID_PAD - HID))).reshape(
            8, own_rows, hidden_size
        )

    blocks = gather(pair, "x", 0).reshape(8, own_parts, HALF)
    blocks = jnp.concatenate(
        [
            blocks[:, :own_rows].reshape(qkv_rows, HALF),
            blocks[:, own_rows],
            blocks[:, own_rows + 1 :].reshape(8 * out_rows, HALF),
        ],
        axis=0,
    )
    gate_up = jnp.concatenate([spread(gate_weight), spread(up_weight)], axis=-1)
    gate_up = gate_up.reshape(RING, 2, own_rows, 2 * hidden_size)
    gate_up = by_core(core, take(gate_up, core, 1), swap(take(gate_up, 1 - core, 1)))
    first = plane_gather(blocks, core, False)
    first, gate_up = together(first, exchange(gate_up, "x", 1))
    gate_up = gate_up.transpose(1, 0, 2, 3).reshape(qkv_rows, 2 * hidden_size)
    down_own = jnp.pad(down_weight, ((0, HID_PAD - HID), (0, 2 * hidden_size - width)))
    packed = jnp.concatenate([gate_up, down_own], axis=0)[None]
    packed = lax.all_gather(packed, ("y", "z"), axis=0, tiled=True)

    def both_sides(mine):
        theirs = swap(mine)
        left = jnp.where(core == 0, mine, theirs).swapaxes(0, 1)
        return left, jnp.where(core == 0, theirs, mine)

    early = qkv_rows + 8
    later = jnp.pad(first[:, :qkv_rows, head_dim:], ((0, 0), (0, 0), (0, OUT_SPLIT - query_half)))
    later = jnp.concatenate([later, first[:, early:, :OUT_SPLIT]], axis=1)
    mine, later = together(plane_gather(first[:, :early, :head_dim], core, True), later)
    left, right = both_sides(mine)
    w_key = left[:, :, :qkv_rows].reshape(width, head_dim)
    w_value = right[:, :, :qkv_rows].reshape(width, head_dim)
    flat_gains = left[:, :, qkv_rows:, :gain_count].reshape(-1).astype(F32)
    gain_attn, gain_post_attn, gain_ffn, gain_post_ffn = (
        flat_gains[n * width : (n + 1) * width] for n in range(4)
    )
    gain_query = flat_gains[4 * width : 4 * width + head_dim]
    gain_key = flat_gains[4 * width + head_dim :]

    own_lengths = take(lengths, core, 0)
    key_count = (BACK + 1) * ROWS
    key_index = (chip - BACK) * ROWS + jnp.arange(key_count, dtype=jnp.int32)
    key_seq, key_pos = layout(own_lengths, key_index)
    own_index, own_seq = key_index[-ROWS:], key_seq[-ROWS:]
    cosine_table, sine_table = rope_tables(key_pos[-ROWS:], head_dim)
    inputs = own_tokens.astype(F32)
    attn_in, attn_pull = jax.vjp(rms_norm, inputs, gain_attn)
    attn_low = attn_in.astype(BF)
    key_raw = product(attn_low, w_key)
    values_low = product(attn_low, w_value).astype(BF)

    def path(raw_vec, gain_vec):
        return rotate(rms_norm(raw_vec, gain_vec), cosine_table[:, None], sine_table[:, None])

    keys, key_pull = jax.vjp(path, key_raw[:, None], gain_key)
    key_value = jnp.concatenate([keys[:, 0].astype(BF), values_low], axis=1)
    key_value, attn_low = together(key_value, attn_low)
    window = [
        lax.ppermute(key_value, ALL, [(i, (i + 2 * by) % 128) for i in range(128)])
        for by in range(BACK, 0, -1)
    ]
    left, right = both_sides(plane_gather(later, core, True))
    query_left = left[:, :, :qkv_rows, :query_half].reshape(width, query_half)
    query_right = right[:, :, :qkv_rows, :query_half].reshape(width, query_half)
    out_left = left[:, :, qkv_rows:].reshape(heads * head_dim, OUT_SPLIT)
    out_right = right[:, :, qkv_rows:, : width - OUT_SPLIT].reshape(
        heads * head_dim, width - OUT_SPLIT
    )
    query_raw = jnp.concatenate(
        [product(attn_low, query_left), product(attn_low, query_right)], axis=1
    ).reshape(ROWS, heads, head_dim)
    queries, query_pull = jax.vjp(path, query_raw, gain_query)
    queries_low = queries.astype(BF).reshape(ROWS, heads * head_dim)
    queries_low, window = together(queries_low, window)
    window = window + [key_value]
    distance = own_index[:, None] - key_index[None, :]
    allowed = (
        (key_index[None, :] >= 0)
        & (distance >= 0)
        & (distance < WINDOW)
        & (own_seq[:, None] == key_seq[None, :])
    )
    bias = jnp.where(allowed, 0.0, NEG).astype(F32)
    mixed_low, probs = attend(queries_low, bias, window)
    attn_out = jnp.concatenate(
        [product(mixed_low, out_left), product(mixed_low, out_right)], axis=1
    )
    post_attn, post_attn_pull = jax.vjp(rms_norm, attn_out, gain_post_attn)
    middle = inputs + post_attn
    ffn_in, ffn_pull = jax.vjp(rms_norm, middle, gain_ffn)

    w_gate_up = packed[:, :qkv_rows].reshape(width, 2 * hidden_size)
    w_down = packed[:, qkv_rows:, :width].reshape(hidden_size, width)
    ffn_low = gather_tokens(ffn_in.astype(BF))

    def feed(rows):
        gate_up_proj = product(rows, w_gate_up)
        hidden, pull = jax.vjp(
            gated_gelu, gate_up_proj[:, :hidden_size], gate_up_proj[:, hidden_size:]
        )
        return hidden.astype(BF), pull

    hidden_low, hidden_pull = zip(*[feed(rows) for rows in ffn_low])
    down_proj = scatter_tokens(*[product(hidden, w_down) for hidden in hidden_low])
    post_ffn, post_ffn_pull = jax.vjp(rms_norm, down_proj, gain_post_ffn)
    activations = from_core((middle + post_ffn).astype(BF))

    upstream = own_cotangent.astype(F32)
    grad_down_f, grad_gain_post_ffn = post_ffn_pull(upstream)
    grad_down_low = gather_tokens(grad_down_f.astype(BF))
    grad_w_down = add_up(map(weight_grad, hidden_low, grad_down_low)).astype(BF)
    down_sums = fold_down(grad_w_down.reshape(16, HID_PAD, width), hidden_size)
    down_sums = plane_blocks(down_sums.reshape(RING, RING, -1, hidden_size), core)
    grad_down_low, down_sums = together(grad_down_low, down_sums)
    down_sums = shifted(down_sums)
    grad_gate_up_low = [
        jnp.concatenate(pull(back_product(rows, w_down)), axis=1).astype(BF)
        for pull, rows in zip(hidden_pull, grad_down_low)
    ]
    grad_ffn_in = scatter_tokens(*[back_product(rows, w_gate_up) for rows in grad_gate_up_low])
    grad_w_gate_up = add_up(map(weight_grad, ffn_low, grad_gate_up_low)).astype(BF)
    gate_up_sums = jnp.concatenate(
        [
            grad_w_gate_up[:, :hidden_size].reshape(16, qkv_rows, hidden_size),
            grad_w_gate_up[:, hidden_size:].reshape(16, qkv_rows, hidden_size),
        ],
        axis=1,
    ).reshape(RING, RING, -1, hidden_size)
    (gate_up_sums,) = together(gate_up_sums)
    gate_up_sums = plane_blocks(gate_up_sums, core)
    grad_ffn_in, gate_up_sums, down_sums = together(grad_ffn_in, gate_up_sums, down_sums)
    gate_up_sums = shifted(gate_up_sums)
    grad_middle_norm, grad_gain_ffn = ffn_pull(grad_ffn_in)
    grad_middle = upstream + grad_middle_norm
    grad_attn_f, grad_gain_post_attn = post_attn_pull(grad_middle)
    grad_attn_low = grad_attn_f.astype(BF)
    grad_mixed = back_product(grad_attn_low[:, :OUT_SPLIT], out_left) + back_product(
        grad_attn_low[:, OUT_SPLIT:], out_right
    )
    (*parts, key_value_grad), grad_queries = attend_back(
        queries_low, probs, grad_mixed.astype(BF), window
    )
    for by in range(1, BACK + 1):
        part = parts[BACK - by]
        part = lax.ppermute(part, ALL, [(i, (i - 2 * by) % 128) for i in range(128)])
        key_value_grad = key_value_grad + part.astype(F32)
    grad_queries = grad_queries.reshape(ROWS, heads, head_dim)
    grad_query_raw, grad_gain_query = query_pull(grad_queries)
    query_grad_low = grad_query_raw.astype(BF).reshape(ROWS, heads * head_dim)
    place = jnp.stack([y, z, core])

    def mine_theirs(left, right):
        return jnp.where(core == 0, left, right), jnp.where(core == 0, right, left)

    sides = mine_theirs(query_grad_low[:, :query_half], query_grad_low[:, query_half:])
    sides = [jnp.pad(side, ((0, 0), (0, OUT_SPLIT - query_half))) for side in sides]
    out_sides = mine_theirs(
        grad_attn_low[:, :OUT_SPLIT],
        jnp.pad(grad_attn_low[:, OUT_SPLIT:], ((0, 0), (0, 2 * OUT_SPLIT - width))),
    )
    mine, theirs = pack(
        pack_out_kernel,
        qkv_rows + 8 * out_rows + 8,
        attn_low,
        mixed_low,
        *(side for pair in zip(sides, out_sides) for side in pair),
    )
    key_value_grad, gate_up_sums, mine, theirs = together(
        key_value_grad, gate_up_sums, mine, theirs
    )
    sums = list(cut(place, mine, swap(theirs)))
    ffn_grads = jnp.concatenate([add_up(gate_up_sums), add_up(down_sums)], axis=1)
    sums, ffn_grads = together(sums, ffn_grads)
    sums = shifted(sums)
    ffn_grads = plane_rest(ffn_grads, core)
    grad_key_raw, grad_gain_key = key_pull(key_value_grad[:, None, :head_dim])
    key_low = grad_key_raw[:, 0].astype(BF)
    value_low = key_value_grad[:, head_dim:].astype(BF)
    grad_attn_in = (
        back_product(query_grad_low[:, :query_half], query_left)
        + back_product(query_grad_low[:, query_half:], query_right)
        + back_product(key_low, w_key)
        + back_product(value_low, w_value)
    )
    grad_inputs_norm, grad_gain_attn = attn_pull(grad_attn_in)
    grad_tokens = grad_middle + grad_inputs_norm
    grad_gains = jnp.concatenate(
        [
            grad_gain_attn,
            grad_gain_post_attn,
            grad_gain_ffn,
            grad_gain_post_ffn,
            grad_gain_query,
            grad_gain_key,
        ]
    ).reshape(16, 8, gain_count)
    grad_gains = jnp.pad(grad_gains, ((0, 0), (0, 0), (0, head_dim - gain_count)))
    mine, theirs = pack(
        pack_kernel, qkv_rows + 8, attn_low, grad_gains, *mine_theirs(key_low, value_low)
    )
    late_sums = list(cut(place, mine, swap(theirs)))
    sums, late_sums, grad_tokens, ffn_grads = together(sums, late_sums, grad_tokens, ffn_grads)
    late_sums = shifted(late_sums)
    back = ffn_grads[: 2 * qkv_rows].astype(BF).reshape(2, RING, 2, own_rows, hidden_size)
    back = [take(back, (x + by) % RING, 1) for by in range(RING)]
    back = back[:1] + [shift(back[by], "x", by) for by in range(1, RING)]
    late_sum = jnp.pad(add_up(late_sums), ((0, 0), (0, 0), (0, OUT_SPLIT - head_dim)))
    total = jnp.concatenate([add_up(sums)[:, :-8], late_sum], axis=1)
    total, grad_tokens, back = together(total, from_core(grad_tokens), back)

    back = jnp.stack([lax.select_n((x - n) % RING, *back) for n in range(RING)], axis=1)
    back = by_core(core, take(back, core, 2), swap(take(back, 1 - core, 2)))
    back = back.reshape(2, 2, RING, own_rows, 16, HID_PAD)[..., :HID]
    back = back.transpose(1, 3, 4, 2, 0, 5).reshape(2, own_rows, 16 * 8 * HID).astype(F32)
    grad_w_down = unfold_down(ffn_grads[None, 2 * qkv_rows :], width)[0, :HID]
    rows = plane_rest(total, core)
    bounds = [0, 8 * out_rows]
    bounds += [bounds[1] + qkv_rows, bounds[1] + 2 * qkv_rows, bounds[1] + 2 * qkv_rows + 8]
    rows = jnp.concatenate(
        [
            rows[low:high].reshape(RING, 2, -1, OUT_SPLIT)
            for low, high in zip(bounds[:-1], bounds[1:])
        ],
        axis=2,
    )
    pair, back, grad_w_down = together(reduce_to_owner(rows, "x", 0), back, grad_w_down)
    sides = by_core(core, take(pair, core, 0), swap(take(pair, 1 - core, 0)))
    kinds = [0, out_rows, out_rows + own_rows, out_rows + 2 * own_rows]
    grad_query = jnp.concatenate(
        [sides[n, kinds[1] : kinds[2], :query_half] for n in range(2)], axis=1
    )
    grad_out = jnp.concatenate(
        [sides[0, : kinds[1]], sides[1, : kinds[1], : width - OUT_SPLIT]], axis=1
    )
    grad_key, grad_value = (sides[n, kinds[2] : kinds[3], :head_dim] for n in range(2))
    grad_gains = sides[0, kinds[3], :gain_count]
    return (
        activations,
        grad_tokens,
        grad_query,
        grad_key,
        grad_value,
        grad_out,
        back[0],
        back[1],
        grad_w_down,
        grad_gains,
    )


def solution(mesh):
    grid = Mesh(mesh.devices.reshape(RING, RING, RING, 2), ALL)
    row = P(ALL, None)
    token = P(None, ALL, None)
    in_specs = (token, P()) + (row,) * 7 + (P(ALL), token)
    out_specs = (token, token) + (row,) * 7 + (P(ALL),)
    return jax.shard_map(body, mesh=grid, in_specs=in_specs, out_specs=out_specs, check_vma=False)
```

```python
import jax
import jax.numpy as jnp
from jax import lax
from jax.experimental import pallas as pl
from jax.experimental.pallas import tpu as pltpu
from jax.sharding import Mesh, PartitionSpec as P

WINDOW = 512
EPS = 1e-06
ROPE_BASE = 10000.0
NEG = -1e30
ALL = ("y", "z", "x", "c")
RING = 4
ROWS = 128
BACK = 4
HALF = 768
OUT_SPLIT = 640
HID = 54
HID_PAD = 56
BF = jnp.bfloat16
F32 = jnp.float32


def rms_norm(values, gain_vec):
    return values * lax.rsqrt(jnp.mean(values * values, axis=-1, keepdims=True) + EPS) * gain_vec


def rotate(values, cosine_table, sine_table):
    half_size = values.shape[-1] // 2
    turned = jnp.concatenate([-values[..., half_size:], values[..., :half_size]], axis=-1)
    return values * cosine_table + turned * sine_table


def rope_tables(position, head_dim):
    frequency_index = jnp.arange(head_dim // 2, dtype=F32)
    inverse = ROPE_BASE ** (-2.0 * frequency_index / head_dim)
    angles = position.astype(F32)[..., None] * inverse
    cosine, sine = jnp.cos(angles), jnp.sin(angles)
    return (jnp.concatenate([cosine, cosine], -1), jnp.concatenate([sine, sine], -1))


def layout(lengths, token_index):
    seq_ends = jnp.cumsum(lengths, axis=-1, dtype=jnp.int32)
    passed = seq_ends[..., None, :] <= token_index[..., :, None]
    seq_id = jnp.sum(passed.astype(jnp.int32), axis=-1, dtype=jnp.int32)
    seq_start = jnp.sum(jnp.where(passed, lengths[..., None, :], 0), axis=-1, dtype=jnp.int32)
    return (seq_id, token_index - seq_start)


def gated_gelu(gate_proj, up_proj):
    return jax.nn.gelu(gate_proj, approximate=True) * up_proj


def product(operand, matrix):
    return jnp.dot(operand, matrix, preferred_element_type=F32)


def weight_grad(operand, grad_rows):
    return lax.dot_general(operand, grad_rows, (((0,), (0,)), ((), ())), preferred_element_type=F32)


def back_product(grad_rows, matrix):
    return lax.dot_general(grad_rows, matrix, (((1,), (1,)), ((), ())), preferred_element_type=F32)


def shift(value, axis, by):
    count = lax.axis_size(axis)
    return lax.ppermute(value, axis, [(i, (i + by) % count) for i in range(count)])


def swap(value):
    return shift(value, "c", 1)


def take(value, index, axis):
    return lax.dynamic_index_in_dim(value, index, axis, keepdims=False)


def gather(value, axis, at):
    me = lax.axis_index(axis)
    shape = value.shape[:at] + (RING,) + value.shape[at:]
    out = jnp.zeros(shape, value.dtype)
    for by in range(RING):
        block = shift(value, axis, by) if by else value
        out = lax.dynamic_update_index_in_dim(out, block, (me - by) % RING, at)
    return out


def exchange(value, axis, at):
    me = lax.axis_index(axis)
    out = jnp.zeros(value.shape, value.dtype)
    for by in range(RING):
        block = take(value, (me + by) % RING, at)
        block = shift(block, axis, by) if by else block
        out = lax.dynamic_update_index_in_dim(out, block, (me - by) % RING, at)
    return out


def reduce_to_owner(value, axis, at):
    me = lax.axis_index(axis)
    total = take(value, me, at).astype(F32)
    for by in range(1, RING):
        block = take(value, (me + by) % RING, at).astype(BF)
        total = total + shift(block, axis, by).astype(F32)
    return total


def plane_shift(value, by, late):
    pairs = []
    for index in range(128):
        y, z, rest, core = index // 32, index // 8 % 4, index % 8, index % 2
        if (core == 0) != late:
            y = (y + by) % RING
        else:
            z = (z + by) % RING
        pairs.append((index, (y * RING + z) * 8 + rest))
    return lax.ppermute(value, ALL, pairs)


def plane_gather(value, core, late):
    me = jnp.where((core == 0) != late, lax.axis_index("y"), lax.axis_index("z"))
    blocks = [value] + [plane_shift(value, by, late) for by in range(1, RING)]
    return in_order(blocks, me)


def in_order(blocks, me):
    out = jnp.zeros((RING,) + blocks[0].shape, blocks[0].dtype)
    for by, block in enumerate(blocks):
        out = lax.dynamic_update_index_in_dim(out, block, (me - by) % RING, 0)
    return out


def plane_blocks(value, core):
    y, z = lax.axis_index("y"), lax.axis_index("z")
    return [
        jnp.where(core == 0, take(value, (y + by) % RING, 0), take(value, (z + by) % RING, 1))
        for by in range(RING)
    ]


def plane_rest(total, core):
    me = jnp.where(core == 0, lax.axis_index("z"), lax.axis_index("y"))
    out = take(total, me, 0).astype(F32)
    for by in range(1, RING):
        part = take(total, (me + by) % RING, 0).astype(BF)
        out = out + plane_shift(part, by, True).astype(F32)
    return out


def shifted(blocks):
    return blocks[:1] + [plane_shift(blocks[by], by, False) for by in range(1, RING)]


def add_up(blocks):
    return sum(block.astype(F32) for block in blocks)


def together(*values):
    return lax.optimization_barrier(values)


def fold_down(down, columns):
    count, _, width = down.shape
    rest = width - columns
    tail = down[:, :, columns:].reshape(count, HID_PAD // 8, 8, rest)
    tail = jnp.pad(tail, ((0, 0), (0, 2), (0, 0), (0, 0))).reshape(count, 3, 3, 8, rest)
    tail = tail.swapaxes(2, 3).reshape(count, 24, 3 * rest)
    tail = jnp.pad(tail, ((0, 0), (0, 0), (0, columns - 3 * rest)))
    return jnp.concatenate([down[:, :, :columns], tail], axis=1)


def unfold_down(folded, width):
    count, _, columns = folded.shape
    rest = width - columns
    tail = folded[:, HID_PAD:, : 3 * rest].reshape(count, 3, 8, 3, rest).swapaxes(2, 3)
    tail = tail.reshape(count, 72, rest)[:, :HID_PAD]
    return jnp.concatenate([folded[:, :HID_PAD], tail], axis=2)


def by_core(core, own, other):
    return jnp.where(core == 0, jnp.stack([own, other]), jnp.stack([other, own]))


def gather_tokens(rows):
    mine = join([rows] + [shift(rows, "x", by) for by in range(1, RING)])
    return mine, swap(mine)


def scatter_tokens(mine, theirs):
    mine = mine + swap(theirs.astype(BF)).astype(F32)
    blocks = mine.reshape(RING, mine.shape[0] // RING, -1)
    total = blocks[0]
    for by in range(1, RING):
        total = total + shift(blocks[by].astype(BF), "x", -by).astype(F32)
    return total


def join_kernel(*refs):
    out = refs[-1]
    for n, block in enumerate(refs[:-1]):
        out[n * ROWS : (n + 1) * ROWS] = block[...]


def join(blocks):
    return pl.pallas_call(
        join_kernel,
        out_shape=jax.ShapeDtypeStruct((len(blocks) * ROWS,) + blocks[0].shape[1:], BF),
        compiler_params=pltpu.CompilerParams(vmem_limit_bytes=16 * 1024 * 1024),
        cost_estimate=pl.CostEstimate(flops=0, bytes_accessed=3 << 20, transcendentals=0),
    )(*blocks)


def matmul(left, right, contract):
    return lax.dot_general(left, right, ((contract[:1], contract[1:]), ((), ())), preferred_element_type=F32)


def attend_kernel(query_ref, bias_ref, *refs):
    blocks, (mixed_ref, probs_ref) = refs[:-2], refs[-2:]
    size = blocks[0].shape[1] // 2
    scale = size ** (-0.5)
    for head in range(query_ref.shape[1] // size):
        columns = slice(head * size, (head + 1) * size)
        query = query_ref[:, columns]
        scores = jnp.concatenate(
            [matmul(query, block[:, :size], (1, 1)) for block in blocks], axis=1
        )
        scores = scores * scale + bias_ref[...]
        weights = jnp.exp(scores - jnp.max(scores, axis=1, keepdims=True))
        probs = weights / jnp.sum(weights, axis=1, keepdims=True)
        probs_ref[head] = probs
        low = probs.astype(BF)
        mixed = sum(
            matmul(low[:, n * ROWS : (n + 1) * ROWS], block[:, size:], (1, 0))
            for n, block in enumerate(blocks)
        )
        mixed_ref[:, columns] = mixed.astype(BF)


def attend_back_kernel(query_ref, probs_ref, grad_ref, *refs):
    count = BACK + 1
    blocks, outs, query_out, total = refs[:count], refs[count:-2], refs[-2], refs[-1]
    size = blocks[0].shape[1] // 2
    scale = size ** (-0.5)
    for head in range(query_ref.shape[1] // size):
        columns = slice(head * size, (head + 1) * size)
        query, grad = query_ref[:, columns], grad_ref[:, columns]
        probs = probs_ref[head]
        grad_probs = jnp.concatenate(
            [matmul(grad, block[:, size:], (1, 1)) for block in blocks], axis=1
        )
        grad_scores = probs * (grad_probs - jnp.sum(probs * grad_probs, axis=1, keepdims=True))
        scores_low, probs_low = grad_scores.astype(BF), probs.astype(BF)
        grad_query = jnp.zeros((ROWS, size), F32)
        for n, block in enumerate(blocks):
            rows = slice(n * ROWS, (n + 1) * ROWS)
            grad_query += matmul(scores_low[:, rows], block[:, :size], (1, 0))
            grad_key = matmul(scores_low[:, rows], query, (0, 0)) * scale
            grad_value = matmul(probs_low[:, rows], grad, (0, 0))
            if head:
                grad_key += total[n, :, :size]
                grad_value += total[n, :, size:]
            total[n, :, :size] = grad_key
            total[n, :, size:] = grad_value
        query_out[:, columns] = grad_query * scale
    for n, out in enumerate(outs):
        out[...] = total[n].astype(out.dtype)


def attend(queries, bias, blocks):
    heads = queries.shape[1] // (blocks[0].shape[1] // 2)
    return pl.pallas_call(
        attend_kernel,
        out_shape=(
            jax.ShapeDtypeStruct(queries.shape, BF),
            jax.ShapeDtypeStruct((heads,) + bias.shape, F32),
        ),
        compiler_params=pltpu.CompilerParams(vmem_limit_bytes=32 * 1024 * 1024),
        cost_estimate=pl.CostEstimate(
            flops=4 * queries.size * bias.shape[1],
            bytes_accessed=4 << 20,
            transcendentals=heads * bias.size,
        ),
    )(queries, bias, *blocks)


def attend_back(queries, probs, grad, blocks):
    shape = blocks[0].shape
    *outs, query_out = pl.pallas_call(
        attend_back_kernel,
        out_shape=tuple(jax.ShapeDtypeStruct(shape, BF) for _ in range(BACK))
        + (jax.ShapeDtypeStruct(shape, F32), jax.ShapeDtypeStruct(queries.shape, F32)),
        scratch_shapes=[pltpu.VMEM((BACK + 1,) + shape, F32)],
        compiler_params=pltpu.CompilerParams(vmem_limit_bytes=32 * 1024 * 1024),
        cost_estimate=pl.CostEstimate(flops=1 << 10, bytes_accessed=1 << 10, transcendentals=0),
    )(queries, probs, grad, *blocks)
    return outs, query_out


def pack_kernel(attn_ref, extra_ref, *refs):
    total = refs[-1]
    groups = 16
    rows = attn_ref.shape[1] // groups
    for columns, out in ((refs[0], refs[2]), (refs[1], refs[3])):
        for n in range(attn_ref.shape[1] // ROWS):
            part = slice(n * ROWS, (n + 1) * ROWS)
            total[part] = matmul(attn_ref[:, part], columns[...], (0, 0))
        for group in range(groups):
            block = jnp.concatenate(
                [total[group * rows : (group + 1) * rows], extra_ref[group]], axis=0
            )
            out[group] = block.astype(out.dtype)


def pack_out_kernel(mixed_ref, attn_ref, *refs):
    total = refs[-1]
    groups = 16
    rows, out_rows = attn_ref.shape[1] // groups, mixed_ref.shape[1] // groups
    sides = ((refs[0], refs[1], refs[4]), (refs[2], refs[3], refs[5]))
    for columns, out_columns, out in sides:
        for n in range(attn_ref.shape[1] // ROWS):
            part = slice(n * ROWS, (n + 1) * ROWS)
            total[part] = matmul(attn_ref[:, part], columns[...], (0, 0))
        blank = jnp.zeros((8, total.shape[1]), F32)
        for group in range(groups):
            block = jnp.concatenate([total[group * rows : (group + 1) * rows], blank], axis=0)
            out[group, out_rows:] = block.astype(out.dtype)
        for n in range(mixed_ref.shape[1] // ROWS):
            part = slice(n * ROWS, (n + 1) * ROWS)
            block = matmul(mixed_ref[:, part], out_columns[...], (0, 0)).astype(out.dtype)
            for k in range(ROWS // out_rows):
                group = n * (ROWS // out_rows) + k
                out[group, :out_rows] = block[k * out_rows : (k + 1) * out_rows]


def pack(kernel, rows, attn_low, other, *columns):
    columns_shape = columns[0].shape[1:]
    shape = (16, rows) + columns_shape
    operands = (attn_low, other) if kernel is pack_kernel else (other, attn_low)
    return pl.pallas_call(
        kernel,
        out_shape=(jax.ShapeDtypeStruct(shape, F32), jax.ShapeDtypeStruct(shape, BF)),
        scratch_shapes=[pltpu.VMEM((attn_low.shape[1],) + columns_shape, F32)],
        compiler_params=pltpu.CompilerParams(vmem_limit_bytes=40 * 1024 * 1024),
        cost_estimate=pl.CostEstimate(flops=1 << 10, bytes_accessed=1 << 10, transcendentals=0),
    )(*operands, *columns)


def cut_kernel(place_ref, mine_ref, other_ref, *outs):
    y, z, core = place_ref[0], place_ref[1], place_ref[2]
    for by, out in enumerate(outs):
        for rest in range(RING):
            group = jnp.where(
                core == 0, (y + by) % RING * RING + rest, rest * RING + (z + by) % RING
            )
            block = mine_ref[group] + other_ref[group].astype(F32)
            out[rest] = block.astype(out.dtype)


def cut(place, mine, other):
    shape = (RING,) + mine.shape[1:]
    vmem = pl.BlockSpec(memory_space=pltpu.VMEM)
    return pl.pallas_call(
        cut_kernel,
        in_specs=[pl.BlockSpec(memory_space=pltpu.SMEM), vmem, vmem],
        out_specs=(vmem,) * RING,
        out_shape=(jax.ShapeDtypeStruct(shape, F32),)
        + tuple(jax.ShapeDtypeStruct(shape, BF) for _ in range(1, RING)),
        compiler_params=pltpu.CompilerParams(vmem_limit_bytes=40 * 1024 * 1024),
        cost_estimate=pl.CostEstimate(flops=1 << 10, bytes_accessed=1 << 10, transcendentals=0),
    )(place, mine, other)


def body(
    tokens,
    lengths,
    query_weight,
    key_weight,
    value_weight,
    output_weight,
    gate_weight,
    up_weight,
    down_weight,
    gains,
    cotangent,
):
    width = tokens.shape[2]
    head_dim = key_weight.shape[1]
    heads = query_weight.shape[1] // head_dim
    y, z, x, core = (lax.axis_index(axis) for axis in ALL)
    group = y * RING + z
    chip = group * RING + x
    own_rows = query_weight.shape[0]
    out_rows = output_weight.shape[0]

    def to_core(value):
        own, other = take(value, core, 0), take(value, 1 - core, 0)
        return by_core(core, own, swap(other)).reshape(ROWS, width)

    def from_core(value):
        parts = value.reshape(2, ROWS // 2, width)
        return by_core(core, take(parts, core, 0), swap(take(parts, 1 - core, 0)))

    own_tokens = to_core(tokens)
    own_cotangent = to_core(cotangent)

    query_half = heads * head_dim // 2
    qkv_left = jnp.concatenate([key_weight, query_weight[:, :query_half]], axis=1)
    qkv_right = jnp.concatenate([value_weight, query_weight[:, query_half:]], axis=1)
    gain_count = gains.shape[0]
    own_parts = own_rows + 1 + out_rows
    gain_row = jnp.pad(gains[None], ((0, 0), (0, HALF - gain_count)))
    out_left = jnp.pad(output_weight[:, :OUT_SPLIT], ((0, 0), (0, HALF - OUT_SPLIT)))
    out_right = jnp.pad(output_weight[:, OUT_SPLIT:], ((0, 0), (0, HALF - width + OUT_SPLIT)))
    sides = jnp.stack(
        [
            jnp.concatenate([qkv_left, gain_row, out_left], axis=0),
            jnp.concatenate([qkv_right, gain_row, out_right], axis=0),
        ]
    )
    pair = by_core(core, take(sides, core, 0), swap(take(sides, 1 - core, 0)))
    qkv_rows = 8 * own_rows
    hidden_size = 16 * HID_PAD

    pair, gate_weight, up_weight = together(pair, gate_weight, up_weight)

    def spread(matrix):
        parts = matrix.reshape(own_rows, 16, 8, HID).transpose(2, 0, 1, 3)
        return jnp.pad(parts, ((0, 0), (0, 0), (0, 0), (0, HID_PAD - HID))).reshape(
            8, own_rows, hidden_size
        )

    blocks = gather(pair, "x", 0).reshape(8, own_parts, HALF)
    blocks = jnp.concatenate(
        [
            blocks[:, :own_rows].reshape(qkv_rows, HALF),
            blocks[:, own_rows],
            blocks[:, own_rows + 1 :].reshape(8 * out_rows, HALF),
        ],
        axis=0,
    )
    gate_up = jnp.concatenate([spread(gate_weight), spread(up_weight)], axis=-1)
    gate_up = gate_up.reshape(RING, 2, own_rows, 2 * hidden_size)
    gate_up = by_core(core, take(gate_up, core, 1), swap(take(gate_up, 1 - core, 1)))
    first = plane_gather(blocks, core, False)
    first, gate_up = together(first, exchange(gate_up, "x", 1))
    gate_up = gate_up.transpose(1, 0, 2, 3).reshape(qkv_rows, 2 * hidden_size)
    down_own = jnp.pad(down_weight, ((0, HID_PAD - HID), (0, 0)))
    side = 2 * hidden_size - width
    beside = jnp.concatenate(
        [
            down_own[40:, :side],
            jnp.pad(down_own[40:, side:], ((0, 8), (0, 2 * side - width))),
        ],
        axis=0,
    )
    down_own = jnp.concatenate([down_own[:40], beside], axis=1)
    packed = jnp.concatenate([gate_up, down_own], axis=0)[None]
    packed = lax.all_gather(packed, ("y", "z"), axis=0, tiled=True)

    def both_sides(mine):
        theirs = swap(mine)
        left = jnp.where(core == 0, mine, theirs).swapaxes(0, 1)
        return left, jnp.where(core == 0, theirs, mine)

    early = qkv_rows + 8
    later = jnp.pad(first[:, :qkv_rows, head_dim:], ((0, 0), (0, 0), (0, OUT_SPLIT - query_half)))
    later = jnp.concatenate([later, first[:, early:, :OUT_SPLIT]], axis=1)
    mine, later = together(plane_gather(first[:, :early, :head_dim], core, True), later)
    left, right = both_sides(mine)
    w_key = left[:, :, :qkv_rows].reshape(width, head_dim)
    w_value = right[:, :, :qkv_rows].reshape(width, head_dim)
    flat_gains = left[:, :, qkv_rows:, :gain_count].reshape(-1).astype(F32)
    gain_attn, gain_post_attn, gain_ffn, gain_post_ffn = (
        flat_gains[n * width : (n + 1) * width] for n in range(4)
    )
    gain_query = flat_gains[4 * width : 4 * width + head_dim]
    gain_key = flat_gains[4 * width + head_dim :]

    own_lengths = take(lengths, core, 0)
    key_count = (BACK + 1) * ROWS
    key_index = (chip - BACK) * ROWS + jnp.arange(key_count, dtype=jnp.int32)
    key_seq, key_pos = layout(own_lengths, key_index)
    own_index, own_seq = key_index[-ROWS:], key_seq[-ROWS:]
    cosine_table, sine_table = rope_tables(key_pos[-ROWS:], head_dim)
    inputs = own_tokens.astype(F32)
    attn_in, attn_pull = jax.vjp(rms_norm, inputs, gain_attn)
    attn_low = attn_in.astype(BF)
    key_raw = product(attn_low, w_key)
    values_low = product(attn_low, w_value).astype(BF)

    def path(raw_vec, gain_vec):
        return rotate(rms_norm(raw_vec, gain_vec), cosine_table[:, None], sine_table[:, None])

    keys, key_pull = jax.vjp(path, key_raw[:, None], gain_key)
    key_value = jnp.concatenate([keys[:, 0].astype(BF), values_low], axis=1)
    key_value, attn_low = together(key_value, attn_low)
    window = [
        lax.ppermute(key_value, ALL, [(i, (i + 2 * by) % 128) for i in range(128)])
        for by in range(BACK, 0, -1)
    ]
    left, right = both_sides(plane_gather(later, core, True))
    query_left = left[:, :, :qkv_rows, :query_half].reshape(width, query_half)
    query_right = right[:, :, :qkv_rows, :query_half].reshape(width, query_half)
    out_left = left[:, :, qkv_rows:].reshape(heads * head_dim, OUT_SPLIT)
    out_right = right[:, :, qkv_rows:, : width - OUT_SPLIT].reshape(
        heads * head_dim, width - OUT_SPLIT
    )
    query_raw = jnp.concatenate(
        [product(attn_low, query_left), product(attn_low, query_right)], axis=1
    ).reshape(ROWS, heads, head_dim)
    queries, query_pull = jax.vjp(path, query_raw, gain_query)
    queries_low = queries.astype(BF).reshape(ROWS, heads * head_dim)
    queries_low, window = together(queries_low, window)
    window = window + [key_value]
    distance = own_index[:, None] - key_index[None, :]
    allowed = (
        (key_index[None, :] >= 0)
        & (distance >= 0)
        & (distance < WINDOW)
        & (own_seq[:, None] == key_seq[None, :])
    )
    bias = jnp.where(allowed, 0.0, NEG).astype(F32)
    mixed_low, probs = attend(queries_low, bias, window)
    attn_out = jnp.concatenate(
        [product(mixed_low, out_left), product(mixed_low, out_right)], axis=1
    )
    post_attn, post_attn_pull = jax.vjp(rms_norm, attn_out, gain_post_attn)
    middle = inputs + post_attn
    ffn_in, ffn_pull = jax.vjp(rms_norm, middle, gain_ffn)

    w_gate_up = packed[:, :qkv_rows].reshape(width, 2 * hidden_size)
    w_down = packed[:, qkv_rows:]
    beside = [w_down[:, :16, width:], w_down[:, 16:32, width : 2 * width - side]]
    w_down = jnp.concatenate([w_down[..., :width], jnp.concatenate(beside, axis=2)], axis=1)
    w_down = w_down.reshape(hidden_size, width)
    ffn_low = gather_tokens(ffn_in.astype(BF))
    first_half, w_gate_up, w_down = together(ffn_low[0], w_gate_up, w_down)
    ffn_low = (first_half, ffn_low[1])

    def feed(rows):
        gate_up_proj = product(rows, w_gate_up)
        hidden, pull = jax.vjp(
            gated_gelu, gate_up_proj[:, :hidden_size], gate_up_proj[:, hidden_size:]
        )
        return hidden.astype(BF), pull

    hidden_low, hidden_pull = zip(*[feed(rows) for rows in ffn_low])
    down_proj = scatter_tokens(*[product(hidden, w_down) for hidden in hidden_low])
    post_ffn, post_ffn_pull = jax.vjp(rms_norm, down_proj, gain_post_ffn)
    activations = from_core((middle + post_ffn).astype(BF))

    upstream = own_cotangent.astype(F32)
    grad_down_f, grad_gain_post_ffn = post_ffn_pull(upstream)
    grad_down_low = gather_tokens(grad_down_f.astype(BF))
    grad_w_down = add_up(map(weight_grad, hidden_low, grad_down_low)).astype(BF)
    down_sums = fold_down(grad_w_down.reshape(16, HID_PAD, width), hidden_size)
    down_sums = plane_blocks(down_sums.reshape(RING, RING, -1, hidden_size), core)
    grad_down_low, down_sums = together(grad_down_low, down_sums)
    down_sums = shifted(down_sums)
    grad_gate_up_low = [
        jnp.concatenate(pull(back_product(rows, w_down)), axis=1).astype(BF)
        for pull, rows in zip(hidden_pull, grad_down_low)
    ]
    grad_ffn_in = scatter_tokens(*[back_product(rows, w_gate_up) for rows in grad_gate_up_low])
    grad_w_gate_up = add_up(map(weight_grad, ffn_low, grad_gate_up_low)).astype(BF)
    gate_up_sums = jnp.concatenate(
        [
            grad_w_gate_up[:, :hidden_size].reshape(16, qkv_rows, hidden_size),
            grad_w_gate_up[:, hidden_size:].reshape(16, qkv_rows, hidden_size),
        ],
        axis=1,
    ).reshape(RING, RING, -1, hidden_size)
    (gate_up_sums,) = together(gate_up_sums)
    gate_up_sums = plane_blocks(gate_up_sums, core)
    grad_ffn_in, gate_up_sums, down_sums = together(grad_ffn_in, gate_up_sums, down_sums)
    gate_up_sums = shifted(gate_up_sums)
    grad_middle_norm, grad_gain_ffn = ffn_pull(grad_ffn_in)
    grad_middle = upstream + grad_middle_norm
    grad_attn_f, grad_gain_post_attn = post_attn_pull(grad_middle)
    grad_attn_low = grad_attn_f.astype(BF)
    grad_mixed = back_product(grad_attn_low[:, :OUT_SPLIT], out_left) + back_product(
        grad_attn_low[:, OUT_SPLIT:], out_right
    )
    (*parts, key_value_grad), grad_queries = attend_back(
        queries_low, probs, grad_mixed.astype(BF), window
    )
    for by in range(1, BACK + 1):
        part = parts[BACK - by]
        part = lax.ppermute(part, ALL, [(i, (i - 2 * by) % 128) for i in range(128)])
        key_value_grad = key_value_grad + part.astype(F32)
    grad_queries = grad_queries.reshape(ROWS, heads, head_dim)
    grad_query_raw, grad_gain_query = query_pull(grad_queries)
    query_grad_low = grad_query_raw.astype(BF).reshape(ROWS, heads * head_dim)
    place = jnp.stack([y, z, core])

    def mine_theirs(left, right):
        return jnp.where(core == 0, left, right), jnp.where(core == 0, right, left)

    sides = mine_theirs(query_grad_low[:, :query_half], query_grad_low[:, query_half:])
    sides = [jnp.pad(side, ((0, 0), (0, OUT_SPLIT - query_half))) for side in sides]
    out_sides = mine_theirs(
        grad_attn_low[:, :OUT_SPLIT],
        jnp.pad(grad_attn_low[:, OUT_SPLIT:], ((0, 0), (0, 2 * OUT_SPLIT - width))),
    )
    mine, theirs = pack(
        pack_out_kernel,
        qkv_rows + 8 * out_rows + 8,
        attn_low,
        mixed_low,
        *(side for pair in zip(sides, out_sides) for side in pair),
    )
    key_value_grad, gate_up_sums, mine, theirs = together(
        key_value_grad, gate_up_sums, mine, theirs
    )
    sums = list(cut(place, mine, swap(theirs)))
    ffn_grads = jnp.concatenate([add_up(gate_up_sums), add_up(down_sums)], axis=1)
    sums, ffn_grads = together(sums, ffn_grads)
    sums = shifted(sums)
    ffn_grads = plane_rest(ffn_grads, core)
    grad_key_raw, grad_gain_key = key_pull(key_value_grad[:, None, :head_dim])
    key_low = grad_key_raw[:, 0].astype(BF)
    value_low = key_value_grad[:, head_dim:].astype(BF)
    grad_attn_in = (
        back_product(query_grad_low[:, :query_half], query_left)
        + back_product(query_grad_low[:, query_half:], query_right)
        + back_product(key_low, w_key)
        + back_product(value_low, w_value)
    )
    grad_inputs_norm, grad_gain_attn = attn_pull(grad_attn_in)
    grad_tokens = grad_middle + grad_inputs_norm
    grad_gains = jnp.concatenate(
        [
            grad_gain_attn,
            grad_gain_post_attn,
            grad_gain_ffn,
            grad_gain_post_ffn,
            grad_gain_query,
            grad_gain_key,
        ]
    ).reshape(16, 8, gain_count)
    grad_gains = jnp.pad(grad_gains, ((0, 0), (0, 0), (0, head_dim - gain_count)))
    mine, theirs = pack(
        pack_kernel, qkv_rows + 8, attn_low, grad_gains, *mine_theirs(key_low, value_low)
    )
    late_sums = list(cut(place, mine, swap(theirs)))
    sums, late_sums, grad_tokens, ffn_grads = together(sums, late_sums, grad_tokens, ffn_grads)
    late_sums = shifted(late_sums)
    back = ffn_grads[: 2 * qkv_rows].astype(BF).reshape(2, RING, 2, own_rows, hidden_size)
    back = [take(back, (x + by) % RING, 1) for by in range(RING)]
    back = back[:1] + [shift(back[by], "x", by) for by in range(1, RING)]
    late_sum = jnp.pad(add_up(late_sums), ((0, 0), (0, 0), (0, OUT_SPLIT - head_dim)))
    total = jnp.concatenate([add_up(sums)[:, :-8], late_sum], axis=1)
    total, grad_tokens, back = together(total, from_core(grad_tokens), back)

    back = jnp.stack([lax.select_n((x - n) % RING, *back) for n in range(RING)], axis=1)
    back = by_core(core, take(back, core, 2), swap(take(back, 1 - core, 2)))
    back = back.reshape(2, 2, RING, own_rows, 16, HID_PAD)[..., :HID]
    back = back.transpose(1, 3, 4, 2, 0, 5).reshape(2, own_rows, 16 * 8 * HID).astype(F32)
    grad_w_down = unfold_down(ffn_grads[None, 2 * qkv_rows :], width)[0, :HID]
    rows = plane_rest(total, core)
    bounds = [0, 8 * out_rows]
    bounds += [bounds[1] + qkv_rows, bounds[1] + 2 * qkv_rows, bounds[1] + 2 * qkv_rows + 8]
    rows = jnp.concatenate(
        [
            rows[low:high].reshape(RING, 2, -1, OUT_SPLIT)
            for low, high in zip(bounds[:-1], bounds[1:])
        ],
        axis=2,
    )
    pair, back, grad_w_down = together(reduce_to_owner(rows, "x", 0), back, grad_w_down)
    sides = by_core(core, take(pair, core, 0), swap(take(pair, 1 - core, 0)))
    kinds = [0, out_rows, out_rows + own_rows, out_rows + 2 * own_rows]
    grad_query = jnp.concatenate(
        [sides[n, kinds[1] : kinds[2], :query_half] for n in range(2)], axis=1
    )
    grad_out = jnp.concatenate(
        [sides[0, : kinds[1]], sides[1, : kinds[1], : width - OUT_SPLIT]], axis=1
    )
    grad_key, grad_value = (sides[n, kinds[2] : kinds[3], :head_dim] for n in range(2))
    grad_gains = sides[0, kinds[3], :gain_count]
    return (
        activations,
        grad_tokens,
        grad_query,
        grad_key,
        grad_value,
        grad_out,
        back[0],
        back[1],
        grad_w_down,
        grad_gains,
    )


def solution(mesh):
    grid = Mesh(mesh.devices.reshape(RING, RING, RING, 2), ALL)
    row = P(ALL, None)
    token = P(None, ALL, None)
    in_specs = (token, P()) + (row,) * 7 + (P(ALL), token)
    out_specs = (token, token) + (row,) * 7 + (P(ALL),)
    return jax.shard_map(body, mesh=grid, in_specs=in_specs, out_specs=out_specs, check_vma=False)
```
